32 devices in a mesh: gx: 8 (over y, x, core), yz: 4 (over z).
Axes of the slice: x: 2, y: 2, z: 4, core: 2. Of those that a mesh axis runs over, the one named last changes fastest.
Arguments:
- design: float32 [32, 64, 128], P('gx', 'yz'), may hold values from 0.2 to 1
- passive: int32 [32, 64, 128], P('gx', 'yz'), may hold values 0 or 1
- support: int32 [32, 64, 128], P('gx', 'yz'), may hold values 0 or 1
- warm_modes: float32 [3, 12, 32, 64, 128], P(None, None, 'gx', 'yz'), may hold values from -6 to 6
Outputs:
- mode_shapes: float32 [3, 12, 32, 64, 128], P(None, None, 'gx', 'yz')
- projected: float32 [12, 12], replicated
The draws below stay inside these ranges and needn't reach their ends.
All inputs are finite; a program needn't handle non-finite values. No bound on the sum of `passive` or of `support` on one device may be relied on, other than what follows from the above.
Results may differ from the reference program's by a relative error of at most 0.0001.
Values sent between devices are 32-bit elements; how exact they have to be, the bound alone decides.
A program may use at most 128 MiB of HBM per device.

```python
import jax
import jax.numpy as jnp
import numpy as np
from jax import lax

MODES = 12
SWEEPS = 4
DEGREE = 2
NX = 32
NY = 64
NZ = 128


def place_ends(entries, key, least, top_value):
    dims = entries.shape
    place = [jax.random.randint(jax.random.fold_in(key, axis), (), 0, dims[axis]) for axis in range(len(dims))]
    entries = entries.at[tuple(place)].set(least)
    longest = dims.index(max(dims))
    place[longest] = (place[longest] + 1) % dims[longest]
    return entries.at[tuple(place)].set(top_value)


def shard_levels(key, shape, pieces, least, top_value):
    def one(axis_at, shards_of):
        heights = jax.random.uniform(jax.random.fold_in(jax.random.fold_in(key, 6), axis_at), (shards_of,), jnp.float32, least / len(pieces), top_value / len(pieces))
        return jnp.repeat(jnp.exp(heights), shape[axis_at] // shards_of).reshape((-1,) + (1,) * (len(shape) - axis_at - 1))

    level = one(*pieces[0])
    for cut in pieces[1:]:
        level = level * one(*cut)
    return level


def normal_values(key, shape, scale, most, shards=(), kind=jnp.bfloat16):
    result = scale * jax.random.normal(key, shape, jnp.float32)
    if shards:
        result = result * shard_levels(key, shape, shards, -0.22, 0.18)
    return jnp.clip(result, -most, most).astype(kind)


def setup_inputs(seed: int = 0) -> dict:
    splits = jax.random.split(jax.random.key(seed), 5)
    return {
        "design": jnp.clip(0.2 + 0.8 * jax.random.uniform(splits[0], (NX, NY, NZ), jnp.float32) ** shard_levels(splits[0], (NX, NY, NZ), ((0, 8), (1, 4)), -0.2, 0.2), 0.2, 1.0),
        "passive": place_ends((jax.random.randint(splits[1], (NX, NY, NZ), 0, 10) < 1).astype(jnp.int32), jax.random.fold_in(splits[1], 1), 0, 1),
        "support": place_ends((jax.random.randint(splits[2], (NX, NY, NZ), 0, 16) < 1).astype(jnp.int32), jax.random.fold_in(splits[2], 1), 0, 1),
        "warm_modes": normal_values(splits[3], (3, MODES, NX, NY, NZ), 1.0, 6.0, ((2, 8), (3, 4)), jnp.float32),
    }


soft_modulus = 0.001
filter_weight = 2.0
cut_ratio = 0.02
highest_precision = lax.Precision.HIGHEST

def element_matrix():
    poisson = 0.3
    lame_first = poisson / ((1.0 + poisson) * (1.0 - 2.0 * poisson))
    lame_shear = 0.5 / (1.0 + poisson)
    elastic = np.zeros((6, 6))
    elastic[:3, :3] = lame_first
    for direction in range(3):
        elastic[direction, direction] += 2.0 * lame_shear
        elastic[direction + 3, direction + 3] = lame_shear
    corner_signs = np.array([[a_side, b_side, c_side] for a_side in (0, 1) for b_side in (0, 1) for c_side in (0, 1)]) * 2.0 - 1.0
    gauss_points = np.array([-1.0, 1.0]) / np.sqrt(3.0)
    stiffness = np.zeros((24, 24))
    for first_point in gauss_points:
        for second_point in gauss_points:
            for third_point in gauss_points:
                natural = np.array([first_point, second_point, third_point])
                gradients = np.zeros((8, 3))
                for corner in range(8):
                    for direction in range(3):
                        product = corner_signs[corner, direction] / 8.0
                        for other in range(3):
                            if other != direction:
                                product = product * (1.0 + corner_signs[corner, other] * natural[other])
                        gradients[corner, direction] = 2.0 * product
                strain = np.zeros((6, 24))
                for corner in range(8):
                    strain[0, corner] = gradients[corner, 0]
                    strain[1, 8 + corner] = gradients[corner, 1]
                    strain[2, 16 + corner] = gradients[corner, 2]
                    strain[3, corner] = gradients[corner, 1]
                    strain[3, 8 + corner] = gradients[corner, 0]
                    strain[4, 8 + corner] = gradients[corner, 2]
                    strain[4, 16 + corner] = gradients[corner, 1]
                    strain[5, corner] = gradients[corner, 2]
                    strain[5, 16 + corner] = gradients[corner, 0]
                stiffness = stiffness + strain.T @ elastic @ strain * 0.125
    return stiffness

def upper_value():
    return 8.0 * float(np.max(np.sum(np.abs(element_matrix()), axis=1)))

def jacobi(extended, design, neighbours, inside):
    padded = jnp.pad(extended, ((0, 0), (0, 0), (1, 1)))
    beside_all = padded[2:, 1:-1, 1:-1] + padded[:-2, 1:-1, 1:-1]
    beside_all = beside_all + padded[1:-1, 2:, 1:-1] + padded[1:-1, :-2, 1:-1]
    beside_all = beside_all + padded[1:-1, 1:-1, 2:] + padded[1:-1, 1:-1, :-2]
    return inside * (design + filter_weight * beside_all) / (1.0 + filter_weight * neighbours)

def neighbour_count(x_global, y_global, depth, x_total, y_total):
    z_global = jnp.arange(depth)
    x_part = (x_global > 0).astype(jnp.float32) + (x_global < x_total - 1).astype(jnp.float32)
    y_part = (y_global > 0).astype(jnp.float32) + (y_global < y_total - 1).astype(jnp.float32)
    z_part = (z_global > 0).astype(jnp.float32) + (z_global < depth - 1).astype(jnp.float32)
    return x_part[:, None, None] + y_part[None, :, None] + z_part[None, None, :]

def nodal_mass(density_ext, x_cells, y_cells, z_cells):
    lumped = jnp.zeros((x_cells, y_cells, z_cells), jnp.float32)
    for x_side in (0, 1):
        for y_side in (0, 1):
            for z_side in (0, 1):
                lumped = lumped + density_ext[1 - x_side:1 - x_side + x_cells, 1 - y_side:1 - y_side + y_cells, 1 - z_side:1 - z_side + z_cells]
    return lumped / 8.0

def node_forces(node_block, moduli):
    stiffness = jnp.asarray(element_matrix(), jnp.float32)
    planes = moduli.shape[0]
    y_cells = moduli.shape[1]
    z_cells = moduli.shape[2]
    columns = node_block.shape[1]

    def add_plane(plane_index, accumulated):
        slab_plane = lax.dynamic_slice_in_dim(node_block, plane_index, 2, axis=2)
        corner_list = []
        for x_side in (0, 1):
            for y_side in (0, 1):
                for z_side in (0, 1):
                    corner_list.append(slab_plane[:, :, x_side, y_side:y_side + y_cells, z_side:z_side + z_cells])
        gathered = jnp.stack(corner_list, axis=1).reshape(24, columns, y_cells, z_cells)
        plane_moduli = lax.dynamic_index_in_dim(moduli, plane_index, 0, keepdims=False)
        element_force = jnp.einsum('ab,bmyz->amyz', stiffness, gathered, precision=highest_precision) * plane_moduli
        element_force = element_force.reshape(3, 8, columns, y_cells, z_cells)
        for x_side in (0, 1):
            spread = jnp.zeros((3, columns, y_cells + 1, z_cells + 1), jnp.float32)
            for y_side in (0, 1):
                for z_side in (0, 1):
                    corner = 4 * x_side + 2 * y_side + z_side
                    spread = spread + jnp.pad(element_force[:, corner], ((0, 0), (0, 0), (y_side, 1 - y_side), (z_side, 1 - z_side)))
            current = lax.dynamic_slice_in_dim(accumulated, plane_index + x_side, 1, axis=2)
            accumulated = lax.dynamic_update_slice_in_dim(accumulated, current + spread[:, :, None], plane_index + x_side, axis=2)
        return accumulated
    return lax.fori_loop(0, planes, add_plane, jnp.zeros(node_block.shape, jnp.float32))

def apply_operator(vectors, scaling, moduli_ext):
    node_block = jnp.pad(scaling * vectors, ((0, 0), (0, 0), (1, 1), (1, 1), (1, 1)))
    forces = node_forces(node_block, moduli_ext)
    return scaling * forces[:, :, 1:-1, 1:-1, 1:-1]

def reference(design, passive, support, warm_modes):
    x_cells, y_cells, z_cells = design.shape
    neighbours = neighbour_count(jnp.arange(x_cells), jnp.arange(y_cells), z_cells, x_cells, y_cells)
    filtered = design
    for sweep_index in range(SWEEPS):
        extended = jnp.pad(filtered, ((1, 1), (1, 1), (0, 0)))
        filtered = jacobi(extended, design, neighbours, 1.0)
    density = jnp.where(passive == 1, jnp.float32(1.0), filtered)
    moduli = soft_modulus + (1.0 - soft_modulus) * density ** 3
    density_ext = jnp.pad(density, ((1, 0), (1, 0), (1, 0)))
    moduli_ext = jnp.pad(moduli, ((1, 0), (1, 0), (1, 0)))
    lumped = nodal_mass(density_ext, x_cells, y_cells, z_cells)
    scaling = (1.0 - support.astype(jnp.float32)) / jnp.sqrt(lumped)
    upper_edge = upper_value()
    lower_edge = cut_ratio * upper_edge
    center_value = 0.5 * (upper_edge + lower_edge)
    half_width = 0.5 * (upper_edge - lower_edge)
    previous = warm_modes * (1.0 - support.astype(jnp.float32))
    latest = (apply_operator(previous, scaling, moduli_ext) - center_value * previous) / half_width
    for degree_index in range(DEGREE - 1):
        following = 2.0 * (apply_operator(latest, scaling, moduli_ext) - center_value * latest) / half_width - previous
        previous = latest
        latest = following
    image = apply_operator(latest, scaling, moduli_ext)
    total_dof = 3.0 * x_cells * y_cells * z_cells
    gram = jnp.einsum('cixyz,cjxyz->ij', latest, latest, precision=highest_precision) / total_dof
    stiff = jnp.einsum('cixyz,cjxyz->ij', latest, image, precision=highest_precision) / total_dof
    lower = jnp.linalg.cholesky(gram)
    inverse = jax.scipy.linalg.solve_triangular(lower, jnp.eye(gram.shape[0], dtype=jnp.float32), lower=True)
    ortho = jnp.einsum('ji,cixyz->cjxyz', inverse, latest, precision=highest_precision)
    projected = jnp.dot(jnp.dot(inverse, stiff, precision=highest_precision), inverse.T, precision=highest_precision)
    return (scaling * ortho, projected)
```

```python
import functools

import jax
import jax.numpy as jnp
import numpy as np
from jax import lax
from jax.experimental import pallas as pl
from jax.experimental.pallas import tpu as pltpu
from jax.sharding import PartitionSpec as P

SWEEPS = 4
SOFT = 0.001
CUT = 0.02
MESH = pl.DeviceIdType.MESH
VMEM = pl.BlockSpec(memory_space=pltpu.VMEM)
HALF = 8
ROWS = 8
REACH = 3
BELOW = 2
ABOVE = 3
LIMIT = 60 * 1024 * 1024


def element_matrix():
    poisson = 0.3
    lame_first = poisson / ((1.0 + poisson) * (1.0 - 2.0 * poisson))
    lame_shear = 0.5 / (1.0 + poisson)
    elastic = np.zeros((6, 6))
    elastic[:3, :3] = lame_first
    for direction in range(3):
        elastic[direction, direction] += 2.0 * lame_shear
        elastic[direction + 3, direction + 3] = lame_shear
    corner_signs = (
        np.array(
            [
                [a_side, b_side, c_side]
                for a_side in (0, 1)
                for b_side in (0, 1)
                for c_side in (0, 1)
            ]
        )
        * 2.0
        - 1.0
    )
    gauss_points = np.array([-1.0, 1.0]) / np.sqrt(3.0)
    stiffness = np.zeros((24, 24))
    for first_point in gauss_points:
        for second_point in gauss_points:
            for third_point in gauss_points:
                natural = np.array([first_point, second_point, third_point])
                gradients = np.zeros((8, 3))
                for corner in range(8):
                    for direction in range(3):
                        product = corner_signs[corner, direction] / 8.0
                        for other in range(3):
                            if other != direction:
                                product = product * (
                                    1.0 + corner_signs[corner, other] * natural[other]
                                )
                        gradients[corner, direction] = 2.0 * product
                strain = np.zeros((6, 24))
                for corner in range(8):
                    strain[0, corner] = gradients[corner, 0]
                    strain[1, 8 + corner] = gradients[corner, 1]
                    strain[2, 16 + corner] = gradients[corner, 2]
                    strain[3, corner] = gradients[corner, 1]
                    strain[3, 8 + corner] = gradients[corner, 0]
                    strain[4, 8 + corner] = gradients[corner, 2]
                    strain[4, 16 + corner] = gradients[corner, 1]
                    strain[5, corner] = gradients[corner, 2]
                    strain[5, 16 + corner] = gradients[corner, 0]
                stiffness = stiffness + strain.T @ elastic @ strain * 0.125
    return stiffness


def upper_value():
    return 8.0 * float(np.max(np.sum(np.abs(element_matrix()), axis=1)))


def edges():
    upper = upper_value()
    lower = CUT * upper
    return 0.5 * (upper + lower), 0.5 * (upper - lower)


def part_of(offset, size, before, after):
    first = max(offset * size, -before)
    stop = min(offset * size + size, size + after)
    return first - offset * size, first + before, stop - first


def offsets_of(x_size):
    hops = -(-(SWEEPS + REACH) // x_size)
    found = []
    for dx in range(-hops, hops + 1):
        for dy in (-1, 0, 1):
            if (dx, dy) != (0, 0):
                found.append((dx, dy))
    return found


def exchange_kernel(counts, sizes, design, passive, support, warm, d_out, p_out, s_out, w_out, send, recv):
    x_size, y_size = sizes
    gx, yz = lax.axis_index("gx"), lax.axis_index("yz")
    offsets = offsets_of(x_size)
    deep = SWEEPS + REACH

    def there(dx, dy):
        x, y = gx + dx, yz + dy
        return (x >= 0) & (x < counts[0]) & (y >= 0) & (y < counts[1])

    barrier = pltpu.get_barrier_semaphore()
    met = jnp.int32(0)
    for dx, dy in offsets:
        ok = there(dx, dy)
        met = met + ok.astype(jnp.int32)

        @pl.when(ok)
        def _():
            pl.semaphore_signal(barrier, inc=1, device_id=(gx + dx, yz + dy), device_id_type=MESH)

    stride = x_size * y_size
    columns = warm.shape[0] // stride
    for x in range(x_size):
        for y in range(y_size):
            w_out[x + BELOW, y + BELOW] = warm[pl.ds(x * y_size + y, columns, stride=stride), :]
    d_out[deep : deep + x_size, ROWS : ROWS + y_size] = design[...]
    p_out[REACH : REACH + x_size, ROWS : ROWS + y_size] = passive[...]
    s_out[REACH : REACH + x_size, ROWS : ROWS + y_size] = support[...]
    pl.semaphore_wait(barrier, met)

    def copies(dx, dy, slot):
        made = []
        fields = [
            (design, d_out, deep, deep, ROWS, ROWS, False),
            (passive, p_out, REACH, REACH, ROWS, ROWS, False),
            (support, s_out, REACH, REACH, ROWS, ROWS, False),
            (w_out, w_out, BELOW, ABOVE, BELOW, ABOVE, True),
        ]
        for at, (source, target, xb, xa, yb, ya, packed) in enumerate(fields):
            xs, xd, xn = part_of(-dx, x_size, xb, xa)
            ys, yd, yn = part_of(-dy, y_size, yb, ya)
            if xn <= 0 or yn <= 0:
                continue
            if packed:
                xs, ys = xs + BELOW, ys + BELOW
            made.append(
                pltpu.make_async_remote_copy(
                    src_ref=source.at[pl.ds(xs, xn), pl.ds(ys, yn)],
                    dst_ref=target.at[pl.ds(xd, xn), pl.ds(yd, yn)],
                    send_sem=send.at[slot, at],
                    recv_sem=recv.at[slot, at],
                    device_id=(gx + dx, yz + dy),
                    device_id_type=MESH,
                )
            )
        return made

    for slot, (dx, dy) in enumerate(offsets):

        @pl.when(there(dx, dy))
        def _():
            for copy in copies(dx, dy, slot):
                copy.start()

    for slot, (dx, dy) in enumerate(offsets):

        @pl.when(there(-dx, -dy))
        def _():
            for copy in copies(dx, dy, slot):
                copy.wait_recv()

    for slot, (dx, dy) in enumerate(offsets):

        @pl.when(there(dx, dy))
        def _():
            for copy in copies(dx, dy, slot):
                copy.wait_send()


def block_kernel(counts, sizes, modes, d_in, p_in, s_in, w_in, y2_out, scale_out, sums_out, fa, fb, dens, mod, scale, y0, y1, us, ud, fs, fd):
    x_size, y_size = sizes
    depth = d_in.shape[-1]
    x_start, y_start = lax.axis_index("gx") * x_size, lax.axis_index("yz") * y_size
    x_total, y_total = counts[0] * x_size, counts[1] * y_size
    deep = SWEEPS + REACH
    rows = y_size + 2 * ROWS
    row_at = lax.broadcasted_iota(jnp.int32, (rows, depth), 0) + (y_start - ROWS)
    lane_at = lax.broadcasted_iota(jnp.int32, (rows, depth), 1)
    y_in = (row_at >= 0) & (row_at < y_total)
    f32 = jnp.float32

    def one(flag):
        return jnp.where(flag, f32(1.0), f32(0.0))

    yz_part = one(row_at > 0) + one(row_at < y_total - 1) + one(lane_at > 0) + one(lane_at < depth - 1)

    def inside(x):
        return y_in & ((x >= 0) & (x < x_total))

    planes = x_size + 2 * deep

    @pl.loop(0, planes)
    def _(p):
        fa[p] = jnp.where(inside(x_start - deep + p), d_in[p], 0.0)

    for sweep in range(SWEEPS):
        old, new = (fa, fb) if sweep % 2 == 0 else (fb, fa)

        @pl.loop(sweep + 1, planes - sweep - 1)
        def _(p):
            x = x_start - deep + p
            here = old[p]
            around = old[p - 1] + old[p + 1]
            around = around + pltpu.roll(here, 1, 0) + pltpu.roll(here, rows - 1, 0)
            around = around + jnp.where(lane_at > 0, pltpu.roll(here, 1, 1), 0.0)
            around = around + jnp.where(lane_at < depth - 1, pltpu.roll(here, depth - 1, 1), 0.0)
            x_part = jnp.where(x > 0, f32(1.0), f32(0.0)) + jnp.where(x < x_total - 1, f32(1.0), f32(0.0))
            value = (d_in[p] + 2.0 * around) / (1.0 + 2.0 * (x_part + yz_part))
            new[p] = jnp.where(inside(x), value, 0.0)

    last = fa if SWEEPS % 2 == 0 else fb

    @pl.loop(0, x_size + 2 * REACH)
    def _(q):
        x = x_start - REACH + q
        ok = inside(x)
        value = jnp.where(p_in[q] == 1, f32(1.0), last[q + SWEEPS])
        dens[q] = jnp.where(ok, value, 0.0)
        mod[q] = jnp.where(ok, SOFT + (1.0 - SOFT) * (value * value * value), 0.0)

    @pl.loop(1, x_size + 2 * REACH)
    def _(q):
        x = x_start - REACH + q
        pair = dens[q - 1] + dens[q]
        pair = pair + pltpu.roll(pair, 1, 0)
        pair = pair + jnp.where(lane_at > 0, pltpu.roll(pair, 1, 1), 0.0)
        ok = inside(x) & (s_in[q] == 0)
        scale[q] = jnp.where(ok, 1.0 / jnp.sqrt(jnp.where(ok, pair, 8.0) * 0.125), 0.0)

    scale_out[...] = scale[REACH : REACH + x_size, ROWS : ROWS + y_size]

    tile = (HALF, depth)
    lane = lax.broadcasted_iota(jnp.int32, tile, 1)
    sub = lax.broadcasted_iota(jnp.int32, tile, 0)
    x_nodes, y_nodes = x_size + BELOW + ABOVE, y_size + BELOW + ABOVE
    to_row = ROWS - BELOW
    to_plane = REACH - BELOW
    halves = -(-modes // HALF)

    def scale_at(i, j):
        return jnp.broadcast_to(scale[i + to_plane, pl.ds(j + to_row, 1), :], tile)

    def ahead(value):
        return jnp.where(lane < depth - 1, pltpu.roll(value, depth - 1, 1), 0.0)

    def behind(value):
        return jnp.where(lane > 0, pltpu.roll(value, 1, 1), 0.0)

    def put_scaled(h, i, j, c, u):
        after = ahead(u)
        us[h, i, j, c] = u + after
        ud[h, i, j, c] = after - u

    @pl.loop(0, x_nodes)
    def _(i):
        @pl.loop(0, y_nodes)
        def _(j):
            sc = scale_at(i, j)
            for h in range(halves):
                count = min(HALF, modes - h * HALF)
                keep = (sc > 0.0) & (sub < count)
                for c in range(3):
                    first = c * modes + h * HALF
                    begin = min(first, 3 * modes - HALF)
                    value = w_in[i, j, begin : begin + HALF, :]
                    if begin != first:
                        value = pltpu.roll(value, HALF - (first - begin), 0)
                    value = jnp.where(keep, value, 0.0)
                    y0[h, i, j, c] = value
                    put_scaled(h, i, j, c, sc * value)

    poisson = 0.3
    lam = poisson / ((1.0 + poisson) * (1.0 - 2.0 * poisson))
    mu = 0.5 / (1.0 + poisson)
    w0, w1, w2 = 1.0 / 16.0, 1.0 / 48.0, 1.0 / 144.0

    def elements(i0, i1, j0, j1):
        def plane(h, i):
            def x_pairs(j):
                found = []
                for c in range(3):
                    s0, s1 = us[h, i, j, c], us[h, i + 1, j, c]
                    d0, d1 = ud[h, i, j, c], ud[h, i + 1, j, c]
                    found += [s0 + s1, s1 - s0, d0 + d1, d1 - d0]
                return found

            def put(j, part):
                for c in range(3):
                    ss, ds, sd, dd = part[4 * c : 4 * c + 4]
                    fs[h, i, j, c] = fs[h, i, j, c] + (ss - ds)
                    fd[h, i, j, c] = fd[h, i, j, c] + (sd - dd)
                    fs[h, i + 1, j, c] = ss + ds
                    fd[h, i + 1, j, c] = sd + dd

            def column(j, carry):
                low, above = carry[:12], carry[12:]
                high = x_pairs(j + 1)
                e = jnp.broadcast_to(mod[i + to_plane, pl.ds(j + to_row, 1), :], tile)
                u = []
                for c in range(3):
                    now = {}
                    for at, (xb, zb) in enumerate(((0, 0), (1, 0), (0, 1), (1, 1))):
                        p, q = low[4 * c + at], high[4 * c + at]
                        now[xb, 0, zb] = q + p
                        now[xb, 1, zb] = q - p
                    u.append(now)
                a, b, w = u
                fa_, fb_, fw_ = {}, {}, {}
                e_shear = e * (mu * w0)
                e_twice = e * (2.0 * mu * w0)
                x_, y_, z_ = (1, 0, 0), (0, 1, 0), (0, 0, 1)
                xy, xz, yz, xyz = (1, 1, 0), (1, 0, 1), (0, 1, 1), (1, 1, 1)
                trace = (e * (lam * w0)) * (a[x_] + b[y_] + w[z_])
                fa_[x_] = trace + e_twice * a[x_]
                fb_[y_] = trace + e_twice * b[y_]
                fw_[z_] = trace + e_twice * w[z_]
                fa_[y_] = fb_[x_] = e_shear * (a[y_] + b[x_])
                fa_[z_] = fw_[x_] = e_shear * (a[z_] + w[x_])
                fb_[z_] = fw_[y_] = e_shear * (b[z_] + w[y_])
                e_plus = e * ((2.0 * lam + 3.0 * mu) * w1 * 0.5)
                e_minus = e * (3.0 * mu * w1 * 0.5)
                for f1, k1, f2, k2, v1, v2 in (
                    (fa_, xy, fw_, yz, a[xy], w[yz]),
                    (fa_, xz, fb_, yz, a[xz], b[yz]),
                    (fb_, xy, fw_, xz, b[xy], w[xz]),
                ):
                    plus, minus = e_plus * (v1 + v2), e_minus * (v1 - v2)
                    f1[k1], f2[k2] = plus + minus, plus - minus
                e_mixed = e * (mu * w1)
                total = a[yz] + b[xz] + w[xy]
                fa_[yz] = e_mixed * (total + a[yz])
                fb_[xz] = e_mixed * (total + b[xz])
                fw_[xy] = e_mixed * (total + w[xy])
                e_last = e * ((lam + 4.0 * mu) * w2)
                for f, v in ((fa_, a), (fb_, b), (fw_, w)):
                    f[xyz] = e_last * v[xyz]
                part, rest = [], []
                for c, f in enumerate((fa_, fb_, fw_)):
                    for at, (xb, zb) in enumerate(((0, 0), (1, 0), (0, 1), (1, 1))):
                        odd = f[xb, 1, zb]
                        if (xb, zb) == (0, 0):
                            part.append(above[4 * c + at] - odd)
                            rest.append(odd)
                        else:
                            even = f[xb, 0, zb]
                            part.append(above[4 * c + at] + (even - odd))
                            rest.append(even + odd)
                put(j, part)
                return tuple(high) + tuple(rest)

            zero = jnp.zeros(tile, f32)
            carry = lax.fori_loop(j0, j1, column, tuple(x_pairs(j0)) + (zero,) * 12)
            put(j1, carry[12:])

        @pl.loop(0, halves)
        def _(h):
            @pl.loop(j0, j1 + 1)
            def _(j):
                for c in range(3):
                    fs[h, i0, j, c] = jnp.zeros(tile, f32)
                    fd[h, i0, j, c] = jnp.zeros(tile, f32)

            @pl.loop(i0, i1)
            def _(i):
                plane(h, i)

    def force(h, i, j, c):
        s, d = fs[h, i, j, c], fd[h, i, j, c]
        return (s - d) + behind(s + d)

    center, width = edges()
    elements(0, x_nodes - 1, 0, y_nodes - 1)

    @pl.loop(1, x_nodes - 1)
    def _(i):
        @pl.loop(1, y_nodes - 1)
        def _(j):
            sc = scale_at(i, j)
            to = sc * (1.0 / width)
            for h in range(halves):
                for c in range(3):
                    value = to * force(h, i, j, c) - (center / width) * y0[h, i, j, c]
                    y1[h, i, j, c] = value
                    put_scaled(h, i, j, c, sc * value)

    elements(1, x_nodes - 2, 1, y_nodes - 2)

    @pl.loop(BELOW, BELOW + x_size + 1)
    def _(i):
        @pl.loop(BELOW, BELOW + y_size + 1)
        def _(j):
            sc = scale_at(i, j)
            to = sc * (2.0 / width)
            for h in range(halves):
                for c in range(3):
                    value = to * force(h, i, j, c) - (2.0 * center / width) * y1[h, i, j, c] - y0[h, i, j, c]
                    y0[h, i, j, c] = value
                    y1[h, i, j, c] = sc * value
                    put_scaled(h, i, j, c, sc * value)

    elements(BELOW, BELOW + x_size, BELOW, BELOW + y_size)

    y2_out[...] = y0[:, BELOW : BELOW + x_size, BELOW : BELOW + y_size]

    def pairs(i_count, j_count, right, left):
        def body(n, total):
            i, j = BELOW + n // j_count, BELOW + n % j_count
            total = list(total)
            for c in range(3):
                values = [left(h, i, j, c) for h in range(halves)]
                for m in range(modes):
                    other = jnp.broadcast_to(right[m // HALF, i, j, c, m % HALF : m % HALF + 1, :], tile)
                    for h in range(halves):
                        total[m * halves + h] = total[m * halves + h] + values[h] * other
            return tuple(total)

        return lax.fori_loop(0, i_count * j_count, body, (jnp.zeros(tile, f32),) * (modes * halves))

    gram = pairs(x_size, y_size, y0, lambda h, i, j, c: y0[h, i, j, c])
    for h in range(halves):
        out = jnp.zeros(tile, f32)
        for m in range(modes):
            out = jnp.where(lane == m, jnp.sum(gram[m * halves + h], axis=1, keepdims=True), out)
        sums_out[h] = out
    stiff = pairs(x_size + 1, y_size + 1, y1, force)
    for h in range(halves):
        out = sums_out[h]
        for m in range(modes):
            out = jnp.where(lane == 32 + m, jnp.sum(stiff[m * halves + h], axis=1, keepdims=True), out)
        sums_out[h] = out * (1.0 / (3.0 * x_total * y_total * depth))


def sum_kernel(counts, part, out, first, second, send, recv):
    gx, yz = lax.axis_index("gx"), lax.axis_index("yz")
    barrier = pltpu.get_barrier_semaphore()
    x_count, y_count = counts
    for d in range(1, x_count):
        pl.semaphore_signal(barrier, inc=1, device_id=(lax.rem(gx + d, x_count), yz), device_id_type=MESH)
    for d in range(1, y_count):
        pl.semaphore_signal(barrier, inc=1, device_id=(gx, lax.rem(yz + d, y_count)), device_id_type=MESH)
    first[gx] = part[...]
    pl.semaphore_wait(barrier, x_count + y_count - 2)

    def gather(slots, me, count, device, base):
        sent = []
        for d in range(1, count):
            copy = pltpu.make_async_remote_copy(
                src_ref=slots.at[me],
                dst_ref=slots.at[me],
                send_sem=send.at[base + d],
                recv_sem=recv.at[base + d],
                device_id=device(lax.rem(me + d, count)),
                device_id_type=MESH,
            )
            copy.start()
            sent.append(copy)
        for d in range(1, count):
            source = lax.rem(me + count - d, count)
            pltpu.make_async_remote_copy(
                src_ref=slots.at[source],
                dst_ref=slots.at[source],
                send_sem=send.at[base + d],
                recv_sem=recv.at[base + d],
                device_id=device(source),
                device_id_type=MESH,
            ).wait_recv()
        for copy in sent:
            copy.wait_send()
        total = slots[0]
        for k in range(1, count):
            total = total + slots[k]
        return total

    if x_count > 1:
        second[yz] = gather(first, gx, x_count, lambda k: (k, yz), 0)
    else:
        second[yz] = first[0]
    out[...] = gather(second, yz, y_count, lambda k: (gx, k), x_count) if y_count > 1 else second[0]


def finish_kernel(sizes, modes, sums, y2, scale, shapes, projected):
    x_size, y_size = sizes
    depth = y2.shape[-1]
    halves = y2.shape[0]
    rows = halves * HALF
    f32 = jnp.float32
    sub = lax.broadcasted_iota(jnp.int32, (rows, depth), 0)
    lane = lax.broadcasted_iota(jnp.int32, (rows, depth), 1)
    work = sums[...].reshape(rows, depth)
    work = jnp.where((lane < 64) & (sub < modes), work, 0.0)
    work = jnp.where((lane == sub + 64) & (sub < modes), 1.0, work)
    for k in range(modes):
        column = jnp.sum(jnp.where(lane == k, work, 0.0), axis=1, keepdims=True)
        row = work[k : k + 1, :]
        root = 1.0 / jnp.sqrt(column[k : k + 1, :])
        row = row * root
        work = jnp.where(sub == k, row, work - jnp.where(sub > k, column * root, 0.0) * row)
    inverse = jnp.where(lane < modes, pltpu.roll(work, depth - 64, 1), 0.0)
    half_done = jnp.where(lane < modes, pltpu.roll(work, depth - 32, 1), 0.0)
    product = lax.dot_general(
        half_done, inverse, (((1,), (1,)), ((), ())), precision=lax.Precision.HIGHEST, preferred_element_type=f32
    )
    projected[...] = product[:modes, :modes]
    columns = []
    for m in range(modes):
        column = jnp.sum(jnp.where(lane == m, inverse, 0.0), axis=1, keepdims=True)
        for h in range(halves):
            columns.append(jnp.broadcast_to(column[h * HALF : (h + 1) * HALF], (HALF, depth)))
    stride = x_size * y_size

    @pl.loop(0, x_size)
    def _(x):
        @pl.loop(0, y_size)
        def _(y):
            sc = jnp.broadcast_to(scale[x, pl.ds(y, 1), :], (HALF, depth))
            for c in range(3):
                total = [jnp.zeros((HALF, depth), f32)] * halves
                for m in range(modes):
                    one = jnp.broadcast_to(y2[m // HALF, x, y, c, m % HALF : m % HALF + 1, :], (HALF, depth))
                    for h in range(m // HALF, halves):
                        total[h] = total[h] + columns[m * halves + h] * one
                for h in range(halves):
                    count = min(HALF, modes - h * HALF)
                    at = (c * modes + h * HALF) * stride + x * y_size + y
                    shapes[pl.ds(at, count, stride=stride), :] = (sc * total[h])[:count]


def on_device(counts, design, passive, support, warm_modes):
    x_size, y_size, depth = design.shape
    sizes = (x_size, y_size)
    modes = warm_modes.shape[1]
    halves = -(-modes // HALF)
    deep = SWEEPS + REACH
    f32 = jnp.float32
    rows = y_size + 2 * ROWS
    x_nodes, y_nodes = x_size + BELOW + ABOVE, y_size + BELOW + ABOVE
    slots = len(offsets_of(x_size))
    warm = warm_modes.reshape(3 * modes * x_size * y_size, depth)
    extended = pl.pallas_call(
        functools.partial(exchange_kernel, counts, sizes),
        out_shape=(
            jax.ShapeDtypeStruct((x_size + 2 * deep, rows, depth), f32),
            jax.ShapeDtypeStruct((x_size + 2 * REACH, rows, depth), jnp.int32),
            jax.ShapeDtypeStruct((x_size + 2 * REACH, rows, depth), jnp.int32),
            jax.ShapeDtypeStruct((x_nodes, y_nodes, 3 * modes, depth), f32),
        ),
        in_specs=[VMEM] * 4,
        out_specs=(VMEM,) * 4,
        scratch_shapes=[pltpu.SemaphoreType.DMA((slots, 4)), pltpu.SemaphoreType.DMA((slots, 4))],
        compiler_params=pltpu.CompilerParams(collective_id=0, has_side_effects=True, vmem_limit_bytes=LIMIT),
        name="halo_exchange",
    )(design, passive, support, warm)
    block = pltpu.VMEM((halves, x_nodes, y_nodes, 3, HALF, depth), f32)
    field = pltpu.VMEM((x_size + 2 * deep, rows, depth), f32)
    short = pltpu.VMEM((x_size + 2 * REACH, rows, depth), f32)
    y2, scale, sums = pl.pallas_call(
        functools.partial(block_kernel, counts, sizes, modes),
        out_shape=(
            jax.ShapeDtypeStruct((halves, x_size, y_size, 3, HALF, depth), f32),
            jax.ShapeDtypeStruct((x_size, y_size, depth), f32),
            jax.ShapeDtypeStruct((halves, HALF, depth), f32),
        ),
        in_specs=[VMEM] * 4,
        out_specs=(VMEM,) * 3,
        scratch_shapes=[field, field, short, short, short] + [block] * 6,
        compiler_params=pltpu.CompilerParams(vmem_limit_bytes=LIMIT),
        name="filter_block",
    )(*extended)
    total = pl.pallas_call(
        functools.partial(sum_kernel, counts),
        out_shape=jax.ShapeDtypeStruct(sums.shape, f32),
        in_specs=[VMEM],
        out_specs=VMEM,
        scratch_shapes=[
            pltpu.VMEM((counts[0],) + sums.shape, f32),
            pltpu.VMEM((counts[1],) + sums.shape, f32),
            pltpu.SemaphoreType.DMA((counts[0] + counts[1],)),
            pltpu.SemaphoreType.DMA((counts[0] + counts[1],)),
        ],
        compiler_params=pltpu.CompilerParams(collective_id=1, has_side_effects=True),
        name="sum_grams",
    )(sums)
    shapes, projected = pl.pallas_call(
        functools.partial(finish_kernel, sizes, modes),
        out_shape=(
            jax.ShapeDtypeStruct(warm.shape, f32),
            jax.ShapeDtypeStruct((modes, modes), f32),
        ),
        in_specs=[VMEM] * 3,
        out_specs=(VMEM, VMEM),
        compiler_params=pltpu.CompilerParams(vmem_limit_bytes=LIMIT),
        name="orthonormal_shapes",
    )(total, y2, scale)
    return shapes.reshape(warm_modes.shape), projected


def solution(mesh):
    counts = (mesh.shape["gx"], mesh.shape["yz"])
    return jax.shard_map(
        functools.partial(on_device, counts),
        mesh=mesh,
        in_specs=(
            P("gx", "yz", None),
            P("gx", "yz", None),
            P("gx", "yz", None),
            P(None, None, "gx", "yz", None),
        ),
        out_specs=(P(None, None, "gx", "yz", None), P()),
        check_vma=False,
    )
```

```python
import functools

import jax
import jax.numpy as jnp
import numpy as np
from jax import lax
from jax.experimental import pallas as pl
from jax.experimental.pallas import tpu as pltpu
from jax.sharding import PartitionSpec as P

SWEEPS = 4
SOFT = 0.001
CUT = 0.02
MESH = pl.DeviceIdType.MESH
VMEM = pl.BlockSpec(memory_space=pltpu.VMEM)
HALF = 8
ROWS = 8
REACH = 3
BELOW = 2
ABOVE = 3
LIMIT = 60 * 1024 * 1024


def element_matrix():
    poisson = 0.3
    lame_first = poisson / ((1.0 + poisson) * (1.0 - 2.0 * poisson))
    lame_shear = 0.5 / (1.0 + poisson)
    elastic = np.zeros((6, 6))
    elastic[:3, :3] = lame_first
    for direction in range(3):
        elastic[direction, direction] += 2.0 * lame_shear
        elastic[direction + 3, direction + 3] = lame_shear
    corner_signs = (
        np.array(
            [
                [a_side, b_side, c_side]
                for a_side in (0, 1)
                for b_side in (0, 1)
                for c_side in (0, 1)
            ]
        )
        * 2.0
        - 1.0
    )
    gauss_points = np.array([-1.0, 1.0]) / np.sqrt(3.0)
    stiffness = np.zeros((24, 24))
    for first_point in gauss_points:
        for second_point in gauss_points:
            for third_point in gauss_points:
                natural = np.array([first_point, second_point, third_point])
                gradients = np.zeros((8, 3))
                for corner in range(8):
                    for direction in range(3):
                        product = corner_signs[corner, direction] / 8.0
                        for other in range(3):
                            if other != direction:
                                product = product * (
                                    1.0 + corner_signs[corner, other] * natural[other]
                                )
                        gradients[corner, direction] = 2.0 * product
                strain = np.zeros((6, 24))
                for corner in range(8):
                    strain[0, corner] = gradients[corner, 0]
                    strain[1, 8 + corner] = gradients[corner, 1]
                    strain[2, 16 + corner] = gradients[corner, 2]
                    strain[3, corner] = gradients[corner, 1]
                    strain[3, 8 + corner] = gradients[corner, 0]
                    strain[4, 8 + corner] = gradients[corner, 2]
                    strain[4, 16 + corner] = gradients[corner, 1]
                    strain[5, corner] = gradients[corner, 2]
                    strain[5, 16 + corner] = gradients[corner, 0]
                stiffness = stiffness + strain.T @ elastic @ strain * 0.125
    return stiffness


def upper_value():
    return 8.0 * float(np.max(np.sum(np.abs(element_matrix()), axis=1)))


def edges():
    upper = upper_value()
    lower = CUT * upper
    return 0.5 * (upper + lower), 0.5 * (upper - lower)


def part_of(offset, size, before, after):
    first = max(offset * size, -before)
    stop = min(offset * size + size, size + after)
    return first - offset * size, first + before, stop - first


def offsets_of(x_size):
    hops = -(-(SWEEPS + REACH) // x_size)
    found = []
    for dx in range(-hops, hops + 1):
        for dy in (-1, 0, 1):
            if (dx, dy) != (0, 0):
                found.append((dx, dy))
    return found


def exchange_kernel(counts, sizes, design, passive, support, warm, d_out, p_out, s_out, w_out, send, recv):
    x_size, y_size = sizes
    gx, yz = lax.axis_index("gx"), lax.axis_index("yz")
    offsets = offsets_of(x_size)
    deep = SWEEPS + REACH

    def there(dx, dy):
        x, y = gx + dx, yz + dy
        return (x >= 0) & (x < counts[0]) & (y >= 0) & (y < counts[1])

    barrier = pltpu.get_barrier_semaphore()
    met = jnp.int32(0)
    for dx, dy in offsets:
        ok = there(dx, dy)
        met = met + ok.astype(jnp.int32)

        @pl.when(ok)
        def _():
            pl.semaphore_signal(barrier, inc=1, device_id=(gx + dx, yz + dy), device_id_type=MESH)

    stride = x_size * y_size
    columns = warm.shape[0] // stride
    for x in range(x_size):
        for y in range(y_size):
            w_out[x + BELOW, y + BELOW] = warm[pl.ds(x * y_size + y, columns, stride=stride), :]
    d_out[deep : deep + x_size, ROWS : ROWS + y_size] = design[...]
    p_out[REACH : REACH + x_size, ROWS : ROWS + y_size] = passive[...]
    s_out[REACH : REACH + x_size, ROWS : ROWS + y_size] = support[...]
    pl.semaphore_wait(barrier, met)

    def copies(dx, dy, slot):
        made = []
        fields = [
            (design, d_out, deep, deep, ROWS, ROWS, False),
            (passive, p_out, REACH, REACH, ROWS, ROWS, False),
            (support, s_out, REACH, REACH, ROWS, ROWS, False),
            (w_out, w_out, BELOW, ABOVE, BELOW, ABOVE, True),
        ]
        for at, (source, target, xb, xa, yb, ya, packed) in enumerate(fields):
            xs, xd, xn = part_of(-dx, x_size, xb, xa)
            ys, yd, yn = part_of(-dy, y_size, yb, ya)
            if xn <= 0 or yn <= 0:
                continue
            if packed:
                xs, ys = xs + BELOW, ys + BELOW
            made.append(
                pltpu.make_async_remote_copy(
                    src_ref=source.at[pl.ds(xs, xn), pl.ds(ys, yn)],
                    dst_ref=target.at[pl.ds(xd, xn), pl.ds(yd, yn)],
                    send_sem=send.at[slot, at],
                    recv_sem=recv.at[slot, at],
                    device_id=(gx + dx, yz + dy),
                    device_id_type=MESH,
                )
            )
        return made

    for slot, (dx, dy) in enumerate(offsets):

        @pl.when(there(dx, dy))
        def _():
            for copy in copies(dx, dy, slot):
                copy.start()

    for slot, (dx, dy) in enumerate(offsets):

        @pl.when(there(-dx, -dy))
        def _():
            for copy in copies(dx, dy, slot):
                copy.wait_recv()

    for slot, (dx, dy) in enumerate(offsets):

        @pl.when(there(dx, dy))
        def _():
            for copy in copies(dx, dy, slot):
                copy.wait_send()


def block_kernel(counts, sizes, modes, d_in, p_in, s_in, w_in, y2_out, scale_out, sums_out, fa, fb, dens, mod, scale, y0, y1, us, ud, fs, fd):
    x_size, y_size = sizes
    depth = d_in.shape[-1]
    x_start, y_start = lax.axis_index("gx") * x_size, lax.axis_index("yz") * y_size
    x_total, y_total = counts[0] * x_size, counts[1] * y_size
    deep = SWEEPS + REACH
    rows = y_size + 2 * ROWS
    row_at = lax.broadcasted_iota(jnp.int32, (rows, depth), 0) + (y_start - ROWS)
    lane_at = lax.broadcasted_iota(jnp.int32, (rows, depth), 1)
    y_in = (row_at >= 0) & (row_at < y_total)
    f32 = jnp.float32

    def one(flag):
        return jnp.where(flag, f32(1.0), f32(0.0))

    yz_part = one(row_at > 0) + one(row_at < y_total - 1) + one(lane_at > 0) + one(lane_at < depth - 1)

    def inside(x):
        return y_in & ((x >= 0) & (x < x_total))

    planes = x_size + 2 * deep

    @pl.loop(0, planes)
    def _(p):
        fa[p] = jnp.where(inside(x_start - deep + p), d_in[p], 0.0)

    for sweep in range(SWEEPS):
        old, new = (fa, fb) if sweep % 2 == 0 else (fb, fa)

        @pl.loop(sweep + 1, planes - sweep - 1)
        def _(p):
            x = x_start - deep + p
            here = old[p]
            around = old[p - 1] + old[p + 1]
            around = around + pltpu.roll(here, 1, 0) + pltpu.roll(here, rows - 1, 0)
            around = around + jnp.where(lane_at > 0, pltpu.roll(here, 1, 1), 0.0)
            around = around + jnp.where(lane_at < depth - 1, pltpu.roll(here, depth - 1, 1), 0.0)
            x_part = jnp.where(x > 0, f32(1.0), f32(0.0)) + jnp.where(x < x_total - 1, f32(1.0), f32(0.0))
            value = (d_in[p] + 2.0 * around) / (1.0 + 2.0 * (x_part + yz_part))
            new[p] = jnp.where(inside(x), value, 0.0)

    last = fa if SWEEPS % 2 == 0 else fb

    @pl.loop(0, x_size + 2 * REACH)
    def _(q):
        x = x_start - REACH + q
        ok = inside(x)
        value = jnp.where(p_in[q] == 1, f32(1.0), last[q + SWEEPS])
        dens[q] = jnp.where(ok, value, 0.0)
        mod[q] = jnp.where(ok, SOFT + (1.0 - SOFT) * (value * value * value), 0.0)

    @pl.loop(1, x_size + 2 * REACH)
    def _(q):
        x = x_start - REACH + q
        pair = dens[q - 1] + dens[q]
        pair = pair + pltpu.roll(pair, 1, 0)
        pair = pair + jnp.where(lane_at > 0, pltpu.roll(pair, 1, 1), 0.0)
        ok = inside(x) & (s_in[q] == 0)
        scale[q] = jnp.where(ok, 1.0 / jnp.sqrt(jnp.where(ok, pair, 8.0) * 0.125), 0.0)

    scale_out[...] = scale[REACH : REACH + x_size, ROWS : ROWS + y_size]

    tile = (HALF, depth)
    lane = lax.broadcasted_iota(jnp.int32, tile, 1)
    sub = lax.broadcasted_iota(jnp.int32, tile, 0)
    x_nodes, y_nodes = x_size + BELOW + ABOVE, y_size + BELOW + ABOVE
    to_row = ROWS - BELOW
    to_plane = REACH - BELOW
    halves = -(-modes // HALF)

    def scale_at(i, j):
        return jnp.broadcast_to(scale[i + to_plane, j + to_row : j + to_row + 1, :], tile)

    def ahead(value):
        return jnp.where(lane < depth - 1, pltpu.roll(value, depth - 1, 1), 0.0)

    def behind(value):
        return jnp.where(lane > 0, pltpu.roll(value, 1, 1), 0.0)

    def put_scaled(h, i, j, c, u):
        after = ahead(u)
        us[h, i, j, c] = u + after
        ud[h, i, j, c] = after - u

    @pl.loop(0, x_nodes)
    def _(i):
        for j in range(y_nodes):
            sc = scale_at(i, j)
            for h in range(halves):
                count = min(HALF, modes - h * HALF)
                keep = (sc > 0.0) & (sub < count)
                for c in range(3):
                    first = c * modes + h * HALF
                    begin = min(first, 3 * modes - HALF)
                    value = w_in[i, j, begin : begin + HALF, :]
                    if begin != first:
                        value = pltpu.roll(value, HALF - (first - begin), 0)
                    value = jnp.where(keep, value, 0.0)
                    y0[h, i, j, c] = value
                    put_scaled(h, i, j, c, sc * value)

    poisson = 0.3
    lam = poisson / ((1.0 + poisson) * (1.0 - 2.0 * poisson))
    mu = 0.5 / (1.0 + poisson)
    w0, w1, w2 = 1.0 / 16.0, 1.0 / 48.0, 1.0 / 144.0

    def elements(i0, i1, j0, j1):
        def plane(h, i):
            def x_pairs(j):
                found = []
                for c in range(3):
                    s0, s1 = us[h, i, j, c], us[h, i + 1, j, c]
                    d0, d1 = ud[h, i, j, c], ud[h, i + 1, j, c]
                    found += [s0 + s1, s1 - s0, d0 + d1, d1 - d0]
                return found

            def put(j, part):
                for c in range(3):
                    ss, ds, sd, dd = part[4 * c : 4 * c + 4]
                    fs[h, i, j, c] = fs[h, i, j, c] + (ss - ds)
                    fd[h, i, j, c] = fd[h, i, j, c] + (sd - dd)
                    fs[h, i + 1, j, c] = ss + ds
                    fd[h, i + 1, j, c] = sd + dd

            def column(j, carry):
                low, above = carry[:12], carry[12:]
                high = x_pairs(j + 1)
                e = jnp.broadcast_to(mod[i + to_plane, j + to_row : j + to_row + 1, :], tile)
                u = []
                for c in range(3):
                    now = {}
                    for at, (xb, zb) in enumerate(((0, 0), (1, 0), (0, 1), (1, 1))):
                        p, q = low[4 * c + at], high[4 * c + at]
                        now[xb, 0, zb] = q + p
                        now[xb, 1, zb] = q - p
                    u.append(now)
                a, b, w = u
                fa_, fb_, fw_ = {}, {}, {}
                e_shear = e * (mu * w0)
                e_twice = e * (2.0 * mu * w0)
                x_, y_, z_ = (1, 0, 0), (0, 1, 0), (0, 0, 1)
                xy, xz, yz, xyz = (1, 1, 0), (1, 0, 1), (0, 1, 1), (1, 1, 1)
                trace = (e * (lam * w0)) * (a[x_] + b[y_] + w[z_])
                fa_[x_] = trace + e_twice * a[x_]
                fb_[y_] = trace + e_twice * b[y_]
                fw_[z_] = trace + e_twice * w[z_]
                fa_[y_] = fb_[x_] = e_shear * (a[y_] + b[x_])
                fa_[z_] = fw_[x_] = e_shear * (a[z_] + w[x_])
                fb_[z_] = fw_[y_] = e_shear * (b[z_] + w[y_])
                e_plus = e * ((2.0 * lam + 3.0 * mu) * w1 * 0.5)
                e_minus = e * (3.0 * mu * w1 * 0.5)
                for f1, k1, f2, k2, v1, v2 in (
                    (fa_, xy, fw_, yz, a[xy], w[yz]),
                    (fa_, xz, fb_, yz, a[xz], b[yz]),
                    (fb_, xy, fw_, xz, b[xy], w[xz]),
                ):
                    plus, minus = e_plus * (v1 + v2), e_minus * (v1 - v2)
                    f1[k1], f2[k2] = plus + minus, plus - minus
                e_mixed = e * (mu * w1)
                total = a[yz] + b[xz] + w[xy]
                fa_[yz] = e_mixed * (total + a[yz])
                fb_[xz] = e_mixed * (total + b[xz])
                fw_[xy] = e_mixed * (total + w[xy])
                e_last = e * ((lam + 4.0 * mu) * w2)
                for f, v in ((fa_, a), (fb_, b), (fw_, w)):
                    f[xyz] = e_last * v[xyz]
                part, rest = [], []
                for c, f in enumerate((fa_, fb_, fw_)):
                    for at, (xb, zb) in enumerate(((0, 0), (1, 0), (0, 1), (1, 1))):
                        odd = f[xb, 1, zb]
                        if (xb, zb) == (0, 0):
                            part.append(above[4 * c + at] - odd)
                            rest.append(odd)
                        else:
                            even = f[xb, 0, zb]
                            part.append(above[4 * c + at] + (even - odd))
                            rest.append(even + odd)
                put(j, part)
                return tuple(high) + tuple(rest)

            zero = jnp.zeros(tile, f32)
            carry = tuple(x_pairs(j0)) + (zero,) * 12
            for j in range(j0, j1):
                carry = column(j, carry)
            put(j1, carry[12:])

        @pl.loop(0, halves)
        def _(h):
            for j in range(j0, j1 + 1):
                for c in range(3):
                    fs[h, i0, j, c] = jnp.zeros(tile, f32)
                    fd[h, i0, j, c] = jnp.zeros(tile, f32)

            @pl.loop(i0, i1)
            def _(i):
                plane(h, i)

    def force(h, i, j, c):
        s, d = fs[h, i, j, c], fd[h, i, j, c]
        return (s - d) + behind(s + d)

    center, width = edges()
    elements(0, x_nodes - 1, 0, y_nodes - 1)

    @pl.loop(1, x_nodes - 1)
    def _(i):
        for j in range(1, y_nodes - 1):
            sc = scale_at(i, j)
            to = sc * (1.0 / width)
            for h in range(halves):
                for c in range(3):
                    value = to * force(h, i, j, c) - (center / width) * y0[h, i, j, c]
                    y1[h, i, j, c] = value
                    put_scaled(h, i, j, c, sc * value)

    elements(1, x_nodes - 2, 1, y_nodes - 2)

    @pl.loop(BELOW, BELOW + x_size + 1)
    def _(i):
        for j in range(BELOW, BELOW + y_size + 1):
            sc = scale_at(i, j)
            to = sc * (2.0 / width)
            for h in range(halves):
                for c in range(3):
                    value = to * force(h, i, j, c) - (2.0 * center / width) * y1[h, i, j, c] - y0[h, i, j, c]
                    y0[h, i, j, c] = value
                    y1[h, i, j, c] = sc * value
                    put_scaled(h, i, j, c, sc * value)

    elements(BELOW, BELOW + x_size, BELOW, BELOW + y_size)

    y2_out[...] = y0[:, BELOW : BELOW + x_size, BELOW : BELOW + y_size]

    def pairs(i_count, j_count, right, left):
        def body(n, total):
            i, j = BELOW + n // j_count, BELOW + n % j_count
            total = list(total)
            for c in range(3):
                values = [left(h, i, j, c) for h in range(halves)]
                for m in range(modes):
                    other = jnp.broadcast_to(right[m // HALF, i, j, c, m % HALF : m % HALF + 1, :], tile)
                    for h in range(halves):
                        total[m * halves + h] = total[m * halves + h] + values[h] * other
            return tuple(total)

        return lax.fori_loop(0, i_count * j_count, body, (jnp.zeros(tile, f32),) * (modes * halves))

    gram = pairs(x_size, y_size, y0, lambda h, i, j, c: y0[h, i, j, c])
    for h in range(halves):
        out = jnp.zeros(tile, f32)
        for m in range(modes):
            out = jnp.where(lane == m, jnp.sum(gram[m * halves + h], axis=1, keepdims=True), out)
        sums_out[h] = out

    @pl.loop(BELOW, BELOW + x_size + 1)
    def _(i):
        for j in range(BELOW, BELOW + y_size + 1):
            for h in range(halves):
                for c in range(3):
                    us[h, i, j, c] = force(h, i, j, c)

    stiff = pairs(x_size + 1, y_size + 1, y1, lambda h, i, j, c: us[h, i, j, c])
    for h in range(halves):
        out = sums_out[h]
        for m in range(modes):
            out = jnp.where(lane == 32 + m, jnp.sum(stiff[m * halves + h], axis=1, keepdims=True), out)
        sums_out[h] = out * (1.0 / (3.0 * x_total * y_total * depth))


def sum_kernel(counts, part, out, first, second, send, recv):
    gx, yz = lax.axis_index("gx"), lax.axis_index("yz")
    barrier = pltpu.get_barrier_semaphore()
    x_count, y_count = counts
    for d in range(1, x_count):
        pl.semaphore_signal(barrier, inc=1, device_id=(lax.rem(gx + d, x_count), yz), device_id_type=MESH)
    for d in range(1, y_count):
        pl.semaphore_signal(barrier, inc=1, device_id=(gx, lax.rem(yz + d, y_count)), device_id_type=MESH)
    first[gx] = part[...]
    pl.semaphore_wait(barrier, x_count + y_count - 2)

    def gather(slots, me, count, device, base):
        sent = []
        for d in range(1, count):
            copy = pltpu.make_async_remote_copy(
                src_ref=slots.at[me],
                dst_ref=slots.at[me],
                send_sem=send.at[base + d],
                recv_sem=recv.at[base + d],
                device_id=device(lax.rem(me + d, count)),
                device_id_type=MESH,
            )
            copy.start()
            sent.append(copy)
        for d in range(1, count):
            source = lax.rem(me + count - d, count)
            pltpu.make_async_remote_copy(
                src_ref=slots.at[source],
                dst_ref=slots.at[source],
                send_sem=send.at[base + d],
                recv_sem=recv.at[base + d],
                device_id=device(source),
                device_id_type=MESH,
            ).wait_recv()
        for copy in sent:
            copy.wait_send()
        total = slots[0]
        for k in range(1, count):
            total = total + slots[k]
        return total

    if x_count > 1:
        second[yz] = gather(first, gx, x_count, lambda k: (k, yz), 0)
    else:
        second[yz] = first[0]
    out[...] = gather(second, yz, y_count, lambda k: (gx, k), x_count) if y_count > 1 else second[0]


def finish_kernel(sizes, modes, sums, y2, scale, shapes, projected):
    x_size, y_size = sizes
    depth = y2.shape[-1]
    halves = y2.shape[0]
    rows = halves * HALF
    f32 = jnp.float32
    sub = lax.broadcasted_iota(jnp.int32, (rows, depth), 0)
    lane = lax.broadcasted_iota(jnp.int32, (rows, depth), 1)
    work = sums[...].reshape(rows, depth)
    work = jnp.where((lane < 64) & (sub < modes), work, 0.0)
    work = jnp.where((lane == sub + 64) & (sub < modes), 1.0, work)
    for k in range(modes):
        column = jnp.sum(jnp.where(lane == k, work, 0.0), axis=1, keepdims=True)
        row = work[k : k + 1, :]
        root = 1.0 / jnp.sqrt(column[k : k + 1, :])
        row = row * root
        work = jnp.where(sub == k, row, work - jnp.where(sub > k, column * root, 0.0) * row)
    inverse = jnp.where(lane < modes, pltpu.roll(work, depth - 64, 1), 0.0)
    half_done = jnp.where(lane < modes, pltpu.roll(work, depth - 32, 1), 0.0)
    product = lax.dot_general(
        half_done, inverse, (((1,), (1,)), ((), ())), precision=lax.Precision.HIGHEST, preferred_element_type=f32
    )
    projected[...] = product[:modes, :modes]
    columns = []
    for m in range(modes):
        column = jnp.sum(jnp.where(lane == m, inverse, 0.0), axis=1, keepdims=True)
        for h in range(halves):
            columns.append(jnp.broadcast_to(column[h * HALF : (h + 1) * HALF], (HALF, depth)))
    stride = x_size * y_size

    @pl.loop(0, x_size)
    def _(x):
        @pl.loop(0, y_size)
        def _(y):
            sc = jnp.broadcast_to(scale[x, pl.ds(y, 1), :], (HALF, depth))
            for c in range(3):
                total = [jnp.zeros((HALF, depth), f32)] * halves
                for m in range(modes):
                    one = jnp.broadcast_to(y2[m // HALF, x, y, c, m % HALF : m % HALF + 1, :], (HALF, depth))
                    for h in range(m // HALF, halves):
                        total[h] = total[h] + columns[m * halves + h] * one
                for h in range(halves):
                    count = min(HALF, modes - h * HALF)
                    at = (c * modes + h * HALF) * stride + x * y_size + y
                    shapes[pl.ds(at, count, stride=stride), :] = (sc * total[h])[:count]


def on_device(counts, design, passive, support, warm_modes):
    x_size, y_size, depth = design.shape
    sizes = (x_size, y_size)
    modes = warm_modes.shape[1]
    halves = -(-modes // HALF)
    deep = SWEEPS + REACH
    f32 = jnp.float32
    rows = y_size + 2 * ROWS
    x_nodes, y_nodes = x_size + BELOW + ABOVE, y_size + BELOW + ABOVE
    slots = len(offsets_of(x_size))
    warm = warm_modes.reshape(3 * modes * x_size * y_size, depth)
    extended = pl.pallas_call(
        functools.partial(exchange_kernel, counts, sizes),
        out_shape=(
            jax.ShapeDtypeStruct((x_size + 2 * deep, rows, depth), f32),
            jax.ShapeDtypeStruct((x_size + 2 * REACH, rows, depth), jnp.int32),
            jax.ShapeDtypeStruct((x_size + 2 * REACH, rows, depth), jnp.int32),
            jax.ShapeDtypeStruct((x_nodes, y_nodes, 3 * modes, depth), f32),
        ),
        in_specs=[VMEM] * 4,
        out_specs=(VMEM,) * 4,
        scratch_shapes=[pltpu.SemaphoreType.DMA((slots, 4)), pltpu.SemaphoreType.DMA((slots, 4))],
        compiler_params=pltpu.CompilerParams(collective_id=0, has_side_effects=True, vmem_limit_bytes=LIMIT),
        name="halo_exchange",
    )(design, passive, support, warm)
    block = pltpu.VMEM((halves, x_nodes, y_nodes, 3, HALF, depth), f32)
    field = pltpu.VMEM((x_size + 2 * deep, rows, depth), f32)
    short = pltpu.VMEM((x_size + 2 * REACH, rows, depth), f32)
    y2, scale, sums = pl.pallas_call(
        functools.partial(block_kernel, counts, sizes, modes),
        out_shape=(
            jax.ShapeDtypeStruct((halves, x_size, y_size, 3, HALF, depth), f32),
            jax.ShapeDtypeStruct((x_size, y_size, depth), f32),
            jax.ShapeDtypeStruct((halves, HALF, depth), f32),
        ),
        in_specs=[VMEM] * 4,
        out_specs=(VMEM,) * 3,
        scratch_shapes=[field, field, short, short, short] + [block] * 6,
        compiler_params=pltpu.CompilerParams(vmem_limit_bytes=LIMIT),
        name="filter_block",
    )(*extended)
    total = pl.pallas_call(
        functools.partial(sum_kernel, counts),
        out_shape=jax.ShapeDtypeStruct(sums.shape, f32),
        in_specs=[VMEM],
        out_specs=VMEM,
        scratch_shapes=[
            pltpu.VMEM((counts[0],) + sums.shape, f32),
            pltpu.VMEM((counts[1],) + sums.shape, f32),
            pltpu.SemaphoreType.DMA((counts[0] + counts[1],)),
            pltpu.SemaphoreType.DMA((counts[0] + counts[1],)),
        ],
        compiler_params=pltpu.CompilerParams(collective_id=1, has_side_effects=True),
        name="sum_grams",
    )(sums)
    shapes, projected = pl.pallas_call(
        functools.partial(finish_kernel, sizes, modes),
        out_shape=(
            jax.ShapeDtypeStruct(warm.shape, f32),
            jax.ShapeDtypeStruct((modes, modes), f32),
        ),
        in_specs=[VMEM] * 3,
        out_specs=(VMEM, VMEM),
        compiler_params=pltpu.CompilerParams(vmem_limit_bytes=LIMIT),
        name="orthonormal_shapes",
    )(total, y2, scale)
    return shapes.reshape(warm_modes.shape), projected


def solution(mesh):
    counts = (mesh.shape["gx"], mesh.shape["yz"])
    return jax.shard_map(
        functools.partial(on_device, counts),
        mesh=mesh,
        in_specs=(
            P("gx", "yz", None),
            P("gx", "yz", None),
            P("gx", "yz", None),
            P(None, None, "gx", "yz", None),
        ),
        out_specs=(P(None, None, "gx", "yz", None), P()),
        check_vma=False,
    )
```

```python
import functools

import jax
import jax.numpy as jnp
import numpy as np
from jax import lax
from jax.experimental import pallas as pl
from jax.experimental.pallas import tpu as pltpu
from jax.sharding import PartitionSpec as P

SWEEPS = 4
SOFT = 0.001
CUT = 0.02
MESH = pl.DeviceIdType.MESH
VMEM = pl.BlockSpec(memory_space=pltpu.VMEM)
HALF = 8
ROWS = 8
REACH = 3
BELOW = 2
ABOVE = 3
LIMIT = 60 * 1024 * 1024


def element_matrix():
    poisson = 0.3
    lame_first = poisson / ((1.0 + poisson) * (1.0 - 2.0 * poisson))
    lame_shear = 0.5 / (1.0 + poisson)
    elastic = np.zeros((6, 6))
    elastic[:3, :3] = lame_first
    for direction in range(3):
        elastic[direction, direction] += 2.0 * lame_shear
        elastic[direction + 3, direction + 3] = lame_shear
    corner_signs = (
        np.array(
            [
                [a_side, b_side, c_side]
                for a_side in (0, 1)
                for b_side in (0, 1)
                for c_side in (0, 1)
            ]
        )
        * 2.0
        - 1.0
    )
    gauss_points = np.array([-1.0, 1.0]) / np.sqrt(3.0)
    stiffness = np.zeros((24, 24))
    for first_point in gauss_points:
        for second_point in gauss_points:
            for third_point in gauss_points:
                natural = np.array([first_point, second_point, third_point])
                gradients = np.zeros((8, 3))
                for corner in range(8):
                    for direction in range(3):
                        product = corner_signs[corner, direction] / 8.0
                        for other in range(3):
                            if other != direction:
                                product = product * (
                                    1.0 + corner_signs[corner, other] * natural[other]
                                )
                        gradients[corner, direction] = 2.0 * product
                strain = np.zeros((6, 24))
                for corner in range(8):
                    strain[0, corner] = gradients[corner, 0]
                    strain[1, 8 + corner] = gradients[corner, 1]
                    strain[2, 16 + corner] = gradients[corner, 2]
                    strain[3, corner] = gradients[corner, 1]
                    strain[3, 8 + corner] = gradients[corner, 0]
                    strain[4, 8 + corner] = gradients[corner, 2]
                    strain[4, 16 + corner] = gradients[corner, 1]
                    strain[5, corner] = gradients[corner, 2]
                    strain[5, 16 + corner] = gradients[corner, 0]
                stiffness = stiffness + strain.T @ elastic @ strain * 0.125
    return stiffness


def upper_value():
    return 8.0 * float(np.max(np.sum(np.abs(element_matrix()), axis=1)))


def edges():
    upper = upper_value()
    lower = CUT * upper
    return 0.5 * (upper + lower), 0.5 * (upper - lower)


def part_of(offset, size, before, after):
    first = max(offset * size, -before)
    stop = min(offset * size + size, size + after)
    return first - offset * size, first + before, stop - first


def offsets_of(x_size):
    hops = -(-(SWEEPS + REACH) // x_size)
    found = []
    for dx in range(-hops, hops + 1):
        for dy in (-1, 0, 1):
            if (dx, dy) != (0, 0):
                found.append((dx, dy))
    return found


def filter_density(counts, sizes, d_in, p_in, s_in, fa, fb, dens, mod, scale):
    x_size, y_size = sizes
    depth = d_in.shape[-1]
    x_start, y_start = lax.axis_index("gx") * x_size, lax.axis_index("yz") * y_size
    x_total, y_total = counts[0] * x_size, counts[1] * y_size
    deep = SWEEPS + REACH
    rows = y_size + 2 * ROWS
    row_at = lax.broadcasted_iota(jnp.int32, (rows, depth), 0) + (y_start - ROWS)
    lane_at = lax.broadcasted_iota(jnp.int32, (rows, depth), 1)
    y_in = (row_at >= 0) & (row_at < y_total)
    f32 = jnp.float32

    def one(flag):
        return jnp.where(flag, f32(1.0), f32(0.0))

    yz_part = one(row_at > 0) + one(row_at < y_total - 1) + one(lane_at > 0) + one(lane_at < depth - 1)

    def inside(x):
        return y_in & ((x >= 0) & (x < x_total))

    planes = x_size + 2 * deep

    @pl.loop(0, planes)
    def _(p):
        fa[p] = jnp.where(inside(x_start - deep + p), d_in[p], 0.0)

    for sweep in range(SWEEPS):
        old, new = (fa, fb) if sweep % 2 == 0 else (fb, fa)

        @pl.loop(sweep + 1, planes - sweep - 1)
        def _(p):
            x = x_start - deep + p
            here = old[p]
            around = old[p - 1] + old[p + 1]
            around = around + pltpu.roll(here, 1, 0) + pltpu.roll(here, rows - 1, 0)
            around = around + jnp.where(lane_at > 0, pltpu.roll(here, 1, 1), 0.0)
            around = around + jnp.where(lane_at < depth - 1, pltpu.roll(here, depth - 1, 1), 0.0)
            x_part = jnp.where(x > 0, f32(1.0), f32(0.0)) + jnp.where(x < x_total - 1, f32(1.0), f32(0.0))
            value = (d_in[p] + 2.0 * around) / (1.0 + 2.0 * (x_part + yz_part))
            new[p] = jnp.where(inside(x), value, 0.0)

    last = fa if SWEEPS % 2 == 0 else fb

    @pl.loop(0, x_size + 2 * REACH)
    def _(q):
        x = x_start - REACH + q
        ok = inside(x)
        value = jnp.where(p_in[q] == 1, f32(1.0), last[q + SWEEPS])
        dens[q] = jnp.where(ok, value, 0.0)
        mod[q] = jnp.where(ok, SOFT + (1.0 - SOFT) * (value * value * value), 0.0)

    @pl.loop(1, x_size + 2 * REACH)
    def _(q):
        x = x_start - REACH + q
        pair = dens[q - 1] + dens[q]
        pair = pair + pltpu.roll(pair, 1, 0)
        pair = pair + jnp.where(lane_at > 0, pltpu.roll(pair, 1, 1), 0.0)
        ok = inside(x) & (s_in[q] == 0)
        scale[q] = jnp.where(ok, 1.0 / jnp.sqrt(jnp.where(ok, pair, 8.0) * 0.125), 0.0)


def block_ops(sizes, scale, mod, y0, y1, us, ud, fs, fd):
    x_size, y_size = sizes
    depth = scale.shape[-1]
    f32 = jnp.float32
    tile = (HALF, depth)
    lane = lax.broadcasted_iota(jnp.int32, tile, 1)
    sub = lax.broadcasted_iota(jnp.int32, tile, 0)
    x_nodes, y_nodes = x_size + BELOW + ABOVE, y_size + BELOW + ABOVE
    to_row = ROWS - BELOW
    to_plane = REACH - BELOW

    def scale_at(i, j):
        return jnp.broadcast_to(scale[i + to_plane, j + to_row : j + to_row + 1, :], tile)

    def ahead(value):
        return jnp.where(lane < depth - 1, pltpu.roll(value, depth - 1, 1), 0.0)

    def behind(value):
        return jnp.where(lane > 0, pltpu.roll(value, 1, 1), 0.0)

    def put_scaled(h, i, j, c, u):
        after = ahead(u)
        us[h, i, j, c] = u + after
        ud[h, i, j, c] = after - u

    poisson = 0.3
    lam = poisson / ((1.0 + poisson) * (1.0 - 2.0 * poisson))
    mu = 0.5 / (1.0 + poisson)
    w0, w1, w2 = 1.0 / 16.0, 1.0 / 48.0, 1.0 / 144.0

    def elements(groups, i0, i1, j0, j1):
        def plane(h, i):
            def x_pairs(j):
                found = []
                for c in range(3):
                    s0, s1 = us[h, i, j, c], us[h, i + 1, j, c]
                    d0, d1 = ud[h, i, j, c], ud[h, i + 1, j, c]
                    found += [s0 + s1, s1 - s0, d0 + d1, d1 - d0]
                return found

            def put(j, part):
                for c in range(3):
                    ss, ds, sd, dd = part[4 * c : 4 * c + 4]
                    fs[h, i, j, c] = fs[h, i, j, c] + (ss - ds)
                    fd[h, i, j, c] = fd[h, i, j, c] + (sd - dd)
                    fs[h, i + 1, j, c] = ss + ds
                    fd[h, i + 1, j, c] = sd + dd

            def column(j, carry):
                low, above = carry[:12], carry[12:]
                high = x_pairs(j + 1)
                e = jnp.broadcast_to(mod[i + to_plane, j + to_row : j + to_row + 1, :], tile)
                u = []
                for c in range(3):
                    now = {}
                    for at, (xb, zb) in enumerate(((0, 0), (1, 0), (0, 1), (1, 1))):
                        p, q = low[4 * c + at], high[4 * c + at]
                        now[xb, 0, zb] = q + p
                        now[xb, 1, zb] = q - p
                    u.append(now)
                a, b, w = u
                fa_, fb_, fw_ = {}, {}, {}
                e_shear = e * (mu * w0)
                e_twice = e * (2.0 * mu * w0)
                x_, y_, z_ = (1, 0, 0), (0, 1, 0), (0, 0, 1)
                xy, xz, yz, xyz = (1, 1, 0), (1, 0, 1), (0, 1, 1), (1, 1, 1)
                trace = (e * (lam * w0)) * (a[x_] + b[y_] + w[z_])
                fa_[x_] = trace + e_twice * a[x_]
                fb_[y_] = trace + e_twice * b[y_]
                fw_[z_] = trace + e_twice * w[z_]
                fa_[y_] = fb_[x_] = e_shear * (a[y_] + b[x_])
                fa_[z_] = fw_[x_] = e_shear * (a[z_] + w[x_])
                fb_[z_] = fw_[y_] = e_shear * (b[z_] + w[y_])
                e_plus = e * ((2.0 * lam + 3.0 * mu) * w1 * 0.5)
                e_minus = e * (3.0 * mu * w1 * 0.5)
                for f1, k1, f2, k2, v1, v2 in (
                    (fa_, xy, fw_, yz, a[xy], w[yz]),
                    (fa_, xz, fb_, yz, a[xz], b[yz]),
                    (fb_, xy, fw_, xz, b[xy], w[xz]),
                ):
                    plus, minus = e_plus * (v1 + v2), e_minus * (v1 - v2)
                    f1[k1], f2[k2] = plus + minus, plus - minus
                e_mixed = e * (mu * w1)
                total = a[yz] + b[xz] + w[xy]
                fa_[yz] = e_mixed * (total + a[yz])
                fb_[xz] = e_mixed * (total + b[xz])
                fw_[xy] = e_mixed * (total + w[xy])
                e_last = e * ((lam + 4.0 * mu) * w2)
                for f, v in ((fa_, a), (fb_, b), (fw_, w)):
                    f[xyz] = e_last * v[xyz]
                part, rest = [], []
                for c, f in enumerate((fa_, fb_, fw_)):
                    for at, (xb, zb) in enumerate(((0, 0), (1, 0), (0, 1), (1, 1))):
                        odd = f[xb, 1, zb]
                        if (xb, zb) == (0, 0):
                            part.append(above[4 * c + at] - odd)
                            rest.append(odd)
                        else:
                            even = f[xb, 0, zb]
                            part.append(above[4 * c + at] + (even - odd))
                            rest.append(even + odd)
                put(j, part)
                return tuple(high) + tuple(rest)

            zero = jnp.zeros(tile, f32)
            carry = tuple(x_pairs(j0)) + (zero,) * 12
            for j in range(j0, j1):
                carry = column(j, carry)
            put(j1, carry[12:])

        @pl.loop(0, groups)
        def _(h):
            for j in range(j0, j1 + 1):
                for c in range(3):
                    fs[h, i0, j, c] = jnp.zeros(tile, f32)
                    fd[h, i0, j, c] = jnp.zeros(tile, f32)

            @pl.loop(i0, i1)
            def _(i):
                plane(h, i)

    def force(h, i, j, c):
        s, d = fs[h, i, j, c], fd[h, i, j, c]
        return (s - d) + behind(s + d)

    def filter_modes(groups, count, w_in):
        @pl.loop(0, x_nodes)
        def _(i):
            for j in range(y_nodes):
                sc = scale_at(i, j)
                for h in range(groups):
                    keep = (sc > 0.0) & (sub < count)
                    for c in range(3):
                        first = c * count
                        begin = min(first, 3 * count - HALF)
                        value = w_in[i, j, begin : begin + HALF, :]
                        if begin != first:
                            value = pltpu.roll(value, HALF - (first - begin), 0)
                        value = jnp.where(keep, value, 0.0)
                        y0[h, i, j, c] = value
                        put_scaled(h, i, j, c, sc * value)

        center, width = edges()
        elements(groups, 0, x_nodes - 1, 0, y_nodes - 1)

        @pl.loop(1, x_nodes - 1)
        def _(i):
            for j in range(1, y_nodes - 1):
                sc = scale_at(i, j)
                to = sc * (1.0 / width)
                for h in range(groups):
                    for c in range(3):
                        value = to * force(h, i, j, c) - (center / width) * y0[h, i, j, c]
                        y1[h, i, j, c] = value
                        put_scaled(h, i, j, c, sc * value)

        elements(groups, 1, x_nodes - 2, 1, y_nodes - 2)

        @pl.loop(BELOW, BELOW + x_size + 1)
        def _(i):
            for j in range(BELOW, BELOW + y_size + 1):
                sc = scale_at(i, j)
                to = sc * (2.0 / width)
                for h in range(groups):
                    for c in range(3):
                        value = to * force(h, i, j, c) - (2.0 * center / width) * y1[h, i, j, c] - y0[h, i, j, c]
                        y0[h, i, j, c] = value
                        y1[h, i, j, c] = sc * value
                        put_scaled(h, i, j, c, sc * value)

    return filter_modes, elements, force, scale_at, put_scaled


def exchange_kernel(counts, sizes, modes, design, passive, support, warm, w_out, mod, scale, y2_out, few, d_out, p_out, s_out, fa, fb, dens, y0, y1, us, ud, fs, fd, send, recv):
    x_size, y_size = sizes
    full = modes // HALF * HALF
    if full == modes:
        full = modes - HALF
    rest = modes - full
    gx, yz = lax.axis_index("gx"), lax.axis_index("yz")
    offsets = offsets_of(x_size)
    deep = SWEEPS + REACH

    def there(dx, dy):
        x, y = gx + dx, yz + dy
        return (x >= 0) & (x < counts[0]) & (y >= 0) & (y < counts[1])

    barrier = pltpu.get_barrier_semaphore()
    met = jnp.int32(0)
    for dx, dy in offsets:
        ok = there(dx, dy)
        met = met + ok.astype(jnp.int32)

        @pl.when(ok)
        def _():
            pl.semaphore_signal(barrier, inc=1, device_id=(gx + dx, yz + dy), device_id_type=MESH)

    stride = x_size * y_size

    def pack(target, first, count):
        for x in range(x_size):
            for y in range(y_size):
                for c in range(3):
                    begin = (c * modes + first) * stride + x * y_size + y
                    target[x + BELOW, y + BELOW, c * count : (c + 1) * count] = warm[pl.ds(begin, count, stride=stride), :]

    pack(few, full, rest)
    d_out[deep : deep + x_size, ROWS : ROWS + y_size] = design[...]
    p_out[REACH : REACH + x_size, ROWS : ROWS + y_size] = passive[...]
    s_out[REACH : REACH + x_size, ROWS : ROWS + y_size] = support[...]
    pl.semaphore_wait(barrier, met)

    def copies(dx, dy, slot, chosen):
        made = []
        fields = [
            (design, d_out, deep, deep, ROWS, ROWS, False),
            (passive, p_out, REACH, REACH, ROWS, ROWS, False),
            (support, s_out, REACH, REACH, ROWS, ROWS, False),
            (few, few, BELOW, ABOVE, BELOW, ABOVE, True),
            (w_out, w_out, BELOW, ABOVE, BELOW, ABOVE, True),
        ]
        for at, (source, target, xb, xa, yb, ya, packed) in enumerate(fields):
            if at not in chosen:
                continue
            xs, xd, xn = part_of(-dx, x_size, xb, xa)
            ys, yd, yn = part_of(-dy, y_size, yb, ya)
            if xn <= 0 or yn <= 0:
                continue
            if packed:
                xs, ys = xs + BELOW, ys + BELOW
            made.append(
                pltpu.make_async_remote_copy(
                    src_ref=source.at[pl.ds(xs, xn), pl.ds(ys, yn)],
                    dst_ref=target.at[pl.ds(xd, xn), pl.ds(yd, yn)],
                    send_sem=send.at[slot, at],
                    recv_sem=recv.at[slot, at],
                    device_id=(gx + dx, yz + dy),
                    device_id_type=MESH,
                )
            )
        return made

    def start(chosen):
        for slot, (dx, dy) in enumerate(offsets):

            @pl.when(there(dx, dy))
            def _():
                for copy in copies(dx, dy, slot, chosen):
                    copy.start()

    def arrived(chosen):
        for slot, (dx, dy) in enumerate(offsets):

            @pl.when(there(-dx, -dy))
            def _():
                for copy in copies(dx, dy, slot, chosen):
                    copy.wait_recv()

    start((0, 1, 2))
    start((3,))
    pack(w_out, 0, full)
    start((4,))
    arrived((0, 1, 2))
    filter_density(counts, sizes, d_out, p_out, s_out, fa, fb, dens, mod, scale)
    arrived((3,))
    filter_modes = block_ops(sizes, scale, mod, y0, y1, us, ud, fs, fd)[0]
    filter_modes(1, rest, few)
    y2_out[...] = y0[0, BELOW : BELOW + x_size + 1, BELOW : BELOW + y_size + 1]
    arrived((4,))
    for slot, (dx, dy) in enumerate(offsets):

        @pl.when(there(dx, dy))
        def _():
            for copy in copies(dx, dy, slot, (0, 1, 2, 3, 4)):
                copy.wait_send()


def block_kernel(counts, sizes, modes, w_in, mod, scale, y2_in, y2_out, scale_out, sums_out, y0, y1, us, ud, fs, fd):
    x_size, y_size = sizes
    depth = scale.shape[-1]
    f32 = jnp.float32
    tile = (HALF, depth)
    lane = lax.broadcasted_iota(jnp.int32, tile, 1)
    halves = -(-modes // HALF)
    x_total, y_total = counts[0] * x_size, counts[1] * y_size
    filter_modes, elements, force, scale_at, put_scaled = block_ops(sizes, scale, mod, y0, y1, us, ud, fs, fd)
    scale_out[...] = scale[REACH : REACH + x_size, ROWS : ROWS + y_size]

    @pl.loop(BELOW, BELOW + x_size + 1)
    def _(i):
        for j in range(BELOW, BELOW + y_size + 1):
            sc = scale_at(i, j)
            for c in range(3):
                value = y2_in[i - BELOW, j - BELOW, c]
                y0[halves - 1, i, j, c] = value
                y1[halves - 1, i, j, c] = sc * value
                put_scaled(halves - 1, i, j, c, sc * value)

    if halves > 1:
        filter_modes(halves - 1, HALF, w_in)
    elements(halves, BELOW, BELOW + x_size, BELOW, BELOW + y_size)

    y2_out[...] = y0[:, BELOW : BELOW + x_size, BELOW : BELOW + y_size]

    def pairs(i_count, j_count, right, left):
        def body(n, total):
            i, j = BELOW + n // j_count, BELOW + n % j_count
            total = list(total)
            for c in range(3):
                values = [left(h, i, j, c) for h in range(halves)]
                for m in range(modes):
                    other = jnp.broadcast_to(right[m // HALF, i, j, c, m % HALF : m % HALF + 1, :], tile)
                    for h in range(halves):
                        total[m * halves + h] = total[m * halves + h] + values[h] * other
            return tuple(total)

        return lax.fori_loop(0, i_count * j_count, body, (jnp.zeros(tile, f32),) * (modes * halves))

    gram = pairs(x_size, y_size, y0, lambda h, i, j, c: y0[h, i, j, c])
    for h in range(halves):
        out = jnp.zeros(tile, f32)
        for m in range(modes):
            out = jnp.where(lane == m, jnp.sum(gram[m * halves + h], axis=1, keepdims=True), out)
        sums_out[h] = out

    @pl.loop(BELOW, BELOW + x_size + 1)
    def _(i):
        for j in range(BELOW, BELOW + y_size + 1):
            for h in range(halves):
                for c in range(3):
                    us[h, i, j, c] = force(h, i, j, c)

    stiff = pairs(x_size + 1, y_size + 1, y1, lambda h, i, j, c: us[h, i, j, c])
    for h in range(halves):
        out = sums_out[h]
        for m in range(modes):
            out = jnp.where(lane == 32 + m, jnp.sum(stiff[m * halves + h], axis=1, keepdims=True), out)
        sums_out[h] = out * (1.0 / (3.0 * x_total * y_total * depth))


def sum_kernel(counts, part, out, first, second, send, recv):
    gx, yz = lax.axis_index("gx"), lax.axis_index("yz")
    barrier = pltpu.get_barrier_semaphore()
    x_count, y_count = counts
    for d in range(1, x_count):
        pl.semaphore_signal(barrier, inc=1, device_id=(lax.rem(gx + d, x_count), yz), device_id_type=MESH)
    for d in range(1, y_count):
        pl.semaphore_signal(barrier, inc=1, device_id=(gx, lax.rem(yz + d, y_count)), device_id_type=MESH)
    first[gx] = part[...]
    pl.semaphore_wait(barrier, x_count + y_count - 2)

    def gather(slots, me, count, device, base):
        sent = []
        for d in range(1, count):
            copy = pltpu.make_async_remote_copy(
                src_ref=slots.at[me],
                dst_ref=slots.at[me],
                send_sem=send.at[base + d],
                recv_sem=recv.at[base + d],
                device_id=device(lax.rem(me + d, count)),
                device_id_type=MESH,
            )
            copy.start()
            sent.append(copy)
        for d in range(1, count):
            source = lax.rem(me + count - d, count)
            pltpu.make_async_remote_copy(
                src_ref=slots.at[source],
                dst_ref=slots.at[source],
                send_sem=send.at[base + d],
                recv_sem=recv.at[base + d],
                device_id=device(source),
                device_id_type=MESH,
            ).wait_recv()
        for copy in sent:
            copy.wait_send()
        total = slots[0]
        for k in range(1, count):
            total = total + slots[k]
        return total

    if x_count > 1:
        second[yz] = gather(first, gx, x_count, lambda k: (k, yz), 0)
    else:
        second[yz] = first[0]
    out[...] = gather(second, yz, y_count, lambda k: (gx, k), x_count) if y_count > 1 else second[0]


def finish_kernel(sizes, modes, sums, y2, scale, shapes, projected):
    x_size, y_size = sizes
    depth = y2.shape[-1]
    halves = y2.shape[0]
    rows = halves * HALF
    f32 = jnp.float32
    sub = lax.broadcasted_iota(jnp.int32, (rows, depth), 0)
    lane = lax.broadcasted_iota(jnp.int32, (rows, depth), 1)
    work = sums[...].reshape(rows, depth)
    work = jnp.where((lane < 64) & (sub < modes), work, 0.0)
    work = jnp.where((lane == sub + 64) & (sub < modes), 1.0, work)
    for k in range(modes):
        column = jnp.sum(jnp.where(lane == k, work, 0.0), axis=1, keepdims=True)
        row = work[k : k + 1, :]
        root = 1.0 / jnp.sqrt(column[k : k + 1, :])
        row = row * root
        work = jnp.where(sub == k, row, work - jnp.where(sub > k, column * root, 0.0) * row)
    inverse = jnp.where(lane < modes, pltpu.roll(work, depth - 64, 1), 0.0)
    half_done = jnp.where(lane < modes, pltpu.roll(work, depth - 32, 1), 0.0)
    product = lax.dot_general(
        half_done, inverse, (((1,), (1,)), ((), ())), precision=lax.Precision.HIGHEST, preferred_element_type=f32
    )
    projected[...] = product[:modes, :modes]
    columns = []
    for m in range(modes):
        column = jnp.sum(jnp.where(lane == m, inverse, 0.0), axis=1, keepdims=True)
        for h in range(halves):
            columns.append(jnp.broadcast_to(column[h * HALF : (h + 1) * HALF], (HALF, depth)))
    stride = x_size * y_size

    @pl.loop(0, x_size)
    def _(x):
        @pl.loop(0, y_size)
        def _(y):
            sc = jnp.broadcast_to(scale[x, pl.ds(y, 1), :], (HALF, depth))
            for c in range(3):
                total = [jnp.zeros((HALF, depth), f32)] * halves
                for m in range(modes):
                    one = jnp.broadcast_to(y2[m // HALF, x, y, c, m % HALF : m % HALF + 1, :], (HALF, depth))
                    for h in range(m // HALF, halves):
                        total[h] = total[h] + columns[m * halves + h] * one
                for h in range(halves):
                    count = min(HALF, modes - h * HALF)
                    at = (c * modes + h * HALF) * stride + x * y_size + y
                    shapes[pl.ds(at, count, stride=stride), :] = (sc * total[h])[:count]


def on_device(counts, design, passive, support, warm_modes):
    x_size, y_size, depth = design.shape
    sizes = (x_size, y_size)
    modes = warm_modes.shape[1]
    halves = -(-modes // HALF)
    rest = modes - (halves - 1) * HALF
    deep = SWEEPS + REACH
    f32 = jnp.float32
    rows = y_size + 2 * ROWS
    x_nodes, y_nodes = x_size + BELOW + ABOVE, y_size + BELOW + ABOVE
    slots = len(offsets_of(x_size))
    warm = warm_modes.reshape(3 * modes * x_size * y_size, depth)
    whole_rows = 3 * (modes - rest)
    field = pltpu.VMEM((x_size + 2 * deep, rows, depth), f32)
    short = (x_size + 2 * REACH, rows, depth)
    one = pltpu.VMEM((1, x_nodes, y_nodes, 3, HALF, depth), f32)
    block = pltpu.VMEM((halves, x_nodes, y_nodes, 3, HALF, depth), f32)
    middle = pl.pallas_call(
        functools.partial(exchange_kernel, counts, sizes, modes),
        out_shape=(
            jax.ShapeDtypeStruct((x_nodes, y_nodes, whole_rows, depth), f32),
            jax.ShapeDtypeStruct(short, f32),
            jax.ShapeDtypeStruct(short, f32),
            jax.ShapeDtypeStruct((x_size + 1, y_size + 1, 3, HALF, depth), f32),
        ),
        in_specs=[VMEM] * 4,
        out_specs=(VMEM,) * 4,
        scratch_shapes=[
            pltpu.VMEM((x_nodes, y_nodes, 3 * rest, depth), f32),
            field,
            pltpu.VMEM(short, jnp.int32),
            pltpu.VMEM(short, jnp.int32),
            field,
            field,
            pltpu.VMEM(short, f32),
        ]
        + [one] * 6
        + [pltpu.SemaphoreType.DMA((slots, 5)), pltpu.SemaphoreType.DMA((slots, 5))],
        compiler_params=pltpu.CompilerParams(collective_id=0, has_side_effects=True, vmem_limit_bytes=LIMIT),
        name="exchange_and_filter",
    )(design, passive, support, warm)
    y2, scale, sums = pl.pallas_call(
        functools.partial(block_kernel, counts, sizes, modes),
        out_shape=(
            jax.ShapeDtypeStruct((halves, x_size, y_size, 3, HALF, depth), f32),
            jax.ShapeDtypeStruct((x_size, y_size, depth), f32),
            jax.ShapeDtypeStruct((halves, HALF, depth), f32),
        ),
        in_specs=[VMEM] * 4,
        out_specs=(VMEM,) * 3,
        scratch_shapes=[block] * 6,
        compiler_params=pltpu.CompilerParams(vmem_limit_bytes=LIMIT),
        name="filter_block",
    )(*middle)
    total = pl.pallas_call(
        functools.partial(sum_kernel, counts),
        out_shape=jax.ShapeDtypeStruct(sums.shape, f32),
        in_specs=[VMEM],
        out_specs=VMEM,
        scratch_shapes=[
            pltpu.VMEM((counts[0],) + sums.shape, f32),
            pltpu.VMEM((counts[1],) + sums.shape, f32),
            pltpu.SemaphoreType.DMA((counts[0] + counts[1],)),
            pltpu.SemaphoreType.DMA((counts[0] + counts[1],)),
        ],
        compiler_params=pltpu.CompilerParams(collective_id=1, has_side_effects=True),
        name="sum_grams",
    )(sums)
    shapes, projected = pl.pallas_call(
        functools.partial(finish_kernel, sizes, modes),
        out_shape=(
            jax.ShapeDtypeStruct(warm.shape, f32),
            jax.ShapeDtypeStruct((modes, modes), f32),
        ),
        in_specs=[VMEM] * 3,
        out_specs=(VMEM, VMEM),
        compiler_params=pltpu.CompilerParams(vmem_limit_bytes=LIMIT),
        name="orthonormal_shapes",
    )(total, y2, scale)
    return shapes.reshape(warm_modes.shape), projected


def solution(mesh):
    counts = (mesh.shape["gx"], mesh.shape["yz"])
    return jax.shard_map(
        functools.partial(on_device, counts),
        mesh=mesh,
        in_specs=(
            P("gx", "yz", None),
            P("gx", "yz", None),
            P("gx", "yz", None),
            P(None, None, "gx", "yz", None),
        ),
        out_specs=(P(None, None, "gx", "yz", None), P()),
        check_vma=False,
    )
```

```python
import functools

import jax
import jax.numpy as jnp
import numpy as np
from jax import lax
from jax.experimental import pallas as pl
from jax.experimental.pallas import tpu as pltpu
from jax.sharding import PartitionSpec as P

SWEEPS = 4
SOFT = 0.001
CUT = 0.02
MESH = pl.DeviceIdType.MESH
VMEM = pl.BlockSpec(memory_space=pltpu.VMEM)
HALF = 8
ROWS = 8
REACH = 3
BELOW = 2
ABOVE = 3
LIMIT = 60 * 1024 * 1024


def element_matrix():
    poisson = 0.3
    lame_first = poisson / ((1.0 + poisson) * (1.0 - 2.0 * poisson))
    lame_shear = 0.5 / (1.0 + poisson)
    elastic = np.zeros((6, 6))
    elastic[:3, :3] = lame_first
    for direction in range(3):
        elastic[direction, direction] += 2.0 * lame_shear
        elastic[direction + 3, direction + 3] = lame_shear
    corner_signs = (
        np.array(
            [
                [a_side, b_side, c_side]
                for a_side in (0, 1)
                for b_side in (0, 1)
                for c_side in (0, 1)
            ]
        )
        * 2.0
        - 1.0
    )
    gauss_points = np.array([-1.0, 1.0]) / np.sqrt(3.0)
    stiffness = np.zeros((24, 24))
    for first_point in gauss_points:
        for second_point in gauss_points:
            for third_point in gauss_points:
                natural = np.array([first_point, second_point, third_point])
                gradients = np.zeros((8, 3))
                for corner in range(8):
                    for direction in range(3):
                        product = corner_signs[corner, direction] / 8.0
                        for other in range(3):
                            if other != direction:
                                product = product * (
                                    1.0 + corner_signs[corner, other] * natural[other]
                                )
                        gradients[corner, direction] = 2.0 * product
                strain = np.zeros((6, 24))
                for corner in range(8):
                    strain[0, corner] = gradients[corner, 0]
                    strain[1, 8 + corner] = gradients[corner, 1]
                    strain[2, 16 + corner] = gradients[corner, 2]
                    strain[3, corner] = gradients[corner, 1]
                    strain[3, 8 + corner] = gradients[corner, 0]
                    strain[4, 8 + corner] = gradients[corner, 2]
                    strain[4, 16 + corner] = gradients[corner, 1]
                    strain[5, corner] = gradients[corner, 2]
                    strain[5, 16 + corner] = gradients[corner, 0]
                stiffness = stiffness + strain.T @ elastic @ strain * 0.125
    return stiffness


def upper_value():
    return 8.0 * float(np.max(np.sum(np.abs(element_matrix()), axis=1)))


def edges():
    upper = upper_value()
    lower = CUT * upper
    return 0.5 * (upper + lower), 0.5 * (upper - lower)


def part_of(offset, size, before, after):
    first = max(offset * size, -before)
    stop = min(offset * size + size, size + after)
    return first - offset * size, first + before, stop - first


def offsets_of(x_size):
    hops = -(-(SWEEPS + REACH) // x_size)
    found = []
    for dx in range(-hops, hops + 1):
        for dy in (-1, 0, 1):
            if (dx, dy) != (0, 0):
                found.append((dx, dy))
    return found


def filter_density(counts, sizes, d_in, p_in, s_in, fa, fb, dens, mod, scale):
    x_size, y_size = sizes
    depth = d_in.shape[-1]
    x_start, y_start = lax.axis_index("gx") * x_size, lax.axis_index("yz") * y_size
    x_total, y_total = counts[0] * x_size, counts[1] * y_size
    deep = SWEEPS + REACH
    rows = y_size + 2 * ROWS
    row_at = lax.broadcasted_iota(jnp.int32, (rows, depth), 0) + (y_start - ROWS)
    lane_at = lax.broadcasted_iota(jnp.int32, (rows, depth), 1)
    y_in = (row_at >= 0) & (row_at < y_total)
    f32 = jnp.float32

    def one(flag):
        return jnp.where(flag, f32(1.0), f32(0.0))

    yz_part = one(row_at > 0) + one(row_at < y_total - 1) + one(lane_at > 0) + one(lane_at < depth - 1)

    def inside(x):
        return y_in & ((x >= 0) & (x < x_total))

    planes = x_size + 2 * deep

    @pl.loop(0, planes)
    def _(p):
        fa[p] = jnp.where(inside(x_start - deep + p), d_in[p], 0.0)

    for sweep in range(SWEEPS):
        old, new = (fa, fb) if sweep % 2 == 0 else (fb, fa)

        @pl.loop(sweep + 1, planes - sweep - 1)
        def _(p):
            x = x_start - deep + p
            here = old[p]
            around = old[p - 1] + old[p + 1]
            around = around + pltpu.roll(here, 1, 0) + pltpu.roll(here, rows - 1, 0)
            around = around + jnp.where(lane_at > 0, pltpu.roll(here, 1, 1), 0.0)
            around = around + jnp.where(lane_at < depth - 1, pltpu.roll(here, depth - 1, 1), 0.0)
            x_part = jnp.where(x > 0, f32(1.0), f32(0.0)) + jnp.where(x < x_total - 1, f32(1.0), f32(0.0))
            value = (d_in[p] + 2.0 * around) / (1.0 + 2.0 * (x_part + yz_part))
            new[p] = jnp.where(inside(x), value, 0.0)

    last = fa if SWEEPS % 2 == 0 else fb

    @pl.loop(0, x_size + 2 * REACH)
    def _(q):
        x = x_start - REACH + q
        ok = inside(x)
        value = jnp.where(p_in[q] == 1, f32(1.0), last[q + SWEEPS])
        dens[q] = jnp.where(ok, value, 0.0)
        mod[q] = jnp.where(ok, SOFT + (1.0 - SOFT) * (value * value * value), 0.0)

    @pl.loop(1, x_size + 2 * REACH)
    def _(q):
        x = x_start - REACH + q
        pair = dens[q - 1] + dens[q]
        pair = pair + pltpu.roll(pair, 1, 0)
        pair = pair + jnp.where(lane_at > 0, pltpu.roll(pair, 1, 1), 0.0)
        ok = inside(x) & (s_in[q] == 0)
        scale[q] = jnp.where(ok, 1.0 / jnp.sqrt(jnp.where(ok, pair, 8.0) * 0.125), 0.0)


def block_ops(sizes, scale, mod, y0, y1, us, ud, fs, fd):
    x_size, y_size = sizes
    depth = scale.shape[-1]
    f32 = jnp.float32
    tile = (HALF, depth)
    lane = lax.broadcasted_iota(jnp.int32, tile, 1)
    sub = lax.broadcasted_iota(jnp.int32, tile, 0)
    x_nodes, y_nodes = x_size + BELOW + ABOVE, y_size + BELOW + ABOVE
    to_row = ROWS - BELOW
    to_plane = REACH - BELOW

    def scale_at(i, j):
        return jnp.broadcast_to(scale[i + to_plane, j + to_row : j + to_row + 1, :], tile)

    def ahead(value):
        return jnp.where(lane < depth - 1, pltpu.roll(value, depth - 1, 1), 0.0)

    def behind(value):
        return jnp.where(lane > 0, pltpu.roll(value, 1, 1), 0.0)

    def put_scaled(h, i, j, c, u):
        after = ahead(u)
        us[h, i, j, c] = u + after
        ud[h, i, j, c] = after - u

    poisson = 0.3
    lam = poisson / ((1.0 + poisson) * (1.0 - 2.0 * poisson))
    mu = 0.5 / (1.0 + poisson)
    w0, w1, w2 = 1.0 / 16.0, 1.0 / 48.0, 1.0 / 144.0

    def elements(groups, i0, i1, j0, j1):
        def plane(h, i):
            def x_pairs(j):
                found = []
                for c in range(3):
                    s0, s1 = us[h, i, j, c], us[h, i + 1, j, c]
                    d0, d1 = ud[h, i, j, c], ud[h, i + 1, j, c]
                    found += [s0 + s1, s1 - s0, d0 + d1, d1 - d0]
                return found

            def put(j, part):
                for c in range(3):
                    ss, ds, sd, dd = part[4 * c : 4 * c + 4]
                    fs[h, i, j, c] = fs[h, i, j, c] + (ss - ds)
                    fd[h, i, j, c] = fd[h, i, j, c] + (sd - dd)
                    fs[h, i + 1, j, c] = ss + ds
                    fd[h, i + 1, j, c] = sd + dd

            def column(j, carry):
                low, above = carry[:12], carry[12:]
                high = x_pairs(j + 1)
                e = jnp.broadcast_to(mod[i + to_plane, j + to_row : j + to_row + 1, :], tile)
                u = []
                for c in range(3):
                    now = {}
                    for at, (xb, zb) in enumerate(((0, 0), (1, 0), (0, 1), (1, 1))):
                        p, q = low[4 * c + at], high[4 * c + at]
                        now[xb, 0, zb] = q + p
                        now[xb, 1, zb] = q - p
                    u.append(now)
                a, b, w = u
                fa_, fb_, fw_ = {}, {}, {}
                e_shear = e * (mu * w0)
                e_twice = e * (2.0 * mu * w0)
                x_, y_, z_ = (1, 0, 0), (0, 1, 0), (0, 0, 1)
                xy, xz, yz, xyz = (1, 1, 0), (1, 0, 1), (0, 1, 1), (1, 1, 1)
                trace = (e * (lam * w0)) * (a[x_] + b[y_] + w[z_])
                fa_[x_] = trace + e_twice * a[x_]
                fb_[y_] = trace + e_twice * b[y_]
                fw_[z_] = trace + e_twice * w[z_]
                fa_[y_] = fb_[x_] = e_shear * (a[y_] + b[x_])
                fa_[z_] = fw_[x_] = e_shear * (a[z_] + w[x_])
                fb_[z_] = fw_[y_] = e_shear * (b[z_] + w[y_])
                e_plus = e * ((2.0 * lam + 3.0 * mu) * w1 * 0.5)
                e_minus = e * (3.0 * mu * w1 * 0.5)
                for f1, k1, f2, k2, v1, v2 in (
                    (fa_, xy, fw_, yz, a[xy], w[yz]),
                    (fa_, xz, fb_, yz, a[xz], b[yz]),
                    (fb_, xy, fw_, xz, b[xy], w[xz]),
                ):
                    plus, minus = e_plus * (v1 + v2), e_minus * (v1 - v2)
                    f1[k1], f2[k2] = plus + minus, plus - minus
                e_mixed = e * (mu * w1)
                total = a[yz] + b[xz] + w[xy]
                fa_[yz] = e_mixed * (total + a[yz])
                fb_[xz] = e_mixed * (total + b[xz])
                fw_[xy] = e_mixed * (total + w[xy])
                e_last = e * ((lam + 4.0 * mu) * w2)
                for f, v in ((fa_, a), (fb_, b), (fw_, w)):
                    f[xyz] = e_last * v[xyz]
                part, rest = [], []
                for c, f in enumerate((fa_, fb_, fw_)):
                    for at, (xb, zb) in enumerate(((0, 0), (1, 0), (0, 1), (1, 1))):
                        odd = f[xb, 1, zb]
                        if (xb, zb) == (0, 0):
                            part.append(above[4 * c + at] - odd)
                            rest.append(odd)
                        else:
                            even = f[xb, 0, zb]
                            part.append(above[4 * c + at] + (even - odd))
                            rest.append(even + odd)
                put(j, part)
                return tuple(high) + tuple(rest)

            zero = jnp.zeros(tile, f32)
            carry = tuple(x_pairs(j0)) + (zero,) * 12
            for j in range(j0, j1):
                carry = column(j, carry)
            put(j1, carry[12:])

        @pl.loop(0, groups)
        def _(h):
            for j in range(j0, j1 + 1):
                for c in range(3):
                    fs[h, i0, j, c] = jnp.zeros(tile, f32)
                    fd[h, i0, j, c] = jnp.zeros(tile, f32)

            @pl.loop(i0, i1)
            def _(i):
                plane(h, i)

    def force(h, i, j, c):
        s, d = fs[h, i, j, c], fd[h, i, j, c]
        return (s - d) + behind(s + d)

    def filter_modes(groups, count, w_in):
        @pl.loop(0, x_nodes)
        def _(i):
            for j in range(y_nodes):
                sc = scale_at(i, j)
                for h in range(groups):
                    keep = (sc > 0.0) & (sub < count)
                    for c in range(3):
                        first = c * count
                        begin = min(first, 3 * count - HALF)
                        value = w_in[i, j, begin : begin + HALF, :]
                        if begin != first:
                            value = pltpu.roll(value, HALF - (first - begin), 0)
                        value = jnp.where(keep, value, 0.0)
                        y0[h, i, j, c] = value
                        put_scaled(h, i, j, c, sc * value)

        center, width = edges()
        elements(groups, 0, x_nodes - 1, 0, y_nodes - 1)

        @pl.loop(1, x_nodes - 1)
        def _(i):
            for j in range(1, y_nodes - 1):
                sc = scale_at(i, j)
                to = sc * (1.0 / width)
                for h in range(groups):
                    for c in range(3):
                        value = to * force(h, i, j, c) - (center / width) * y0[h, i, j, c]
                        y1[h, i, j, c] = value
                        put_scaled(h, i, j, c, sc * value)

        elements(groups, 1, x_nodes - 2, 1, y_nodes - 2)

        @pl.loop(BELOW, BELOW + x_size + 1)
        def _(i):
            for j in range(BELOW, BELOW + y_size + 1):
                sc = scale_at(i, j)
                to = sc * (2.0 / width)
                for h in range(groups):
                    for c in range(3):
                        value = to * force(h, i, j, c) - (2.0 * center / width) * y1[h, i, j, c] - y0[h, i, j, c]
                        y0[h, i, j, c] = value
                        y1[h, i, j, c] = sc * value
                        put_scaled(h, i, j, c, sc * value)

    return filter_modes, elements, force


def exchange_kernel(counts, sizes, modes, design, passive, support, warm, w_out, mod, scale, y2_out, force_out, few, d_out, p_out, s_out, fa, fb, dens, y0, y1, us, ud, fs, fd, send, recv):
    x_size, y_size = sizes
    full = modes // HALF * HALF
    if full == modes:
        full = modes - HALF
    rest = modes - full
    gx, yz = lax.axis_index("gx"), lax.axis_index("yz")
    offsets = offsets_of(x_size)
    deep = SWEEPS + REACH

    def there(dx, dy):
        x, y = gx + dx, yz + dy
        return (x >= 0) & (x < counts[0]) & (y >= 0) & (y < counts[1])

    barrier = pltpu.get_barrier_semaphore()
    met = jnp.int32(0)
    for dx, dy in offsets:
        ok = there(dx, dy)
        met = met + ok.astype(jnp.int32)

        @pl.when(ok)
        def _():
            pl.semaphore_signal(barrier, inc=1, device_id=(gx + dx, yz + dy), device_id_type=MESH)

    stride = x_size * y_size

    def pack(target, first, count):
        for x in range(x_size):
            for y in range(y_size):
                for c in range(3):
                    begin = (c * modes + first) * stride + x * y_size + y
                    target[x + BELOW, y + BELOW, c * count : (c + 1) * count] = warm[pl.ds(begin, count, stride=stride), :]

    pack(few, full, rest)
    d_out[deep : deep + x_size, ROWS : ROWS + y_size] = design[...]
    p_out[REACH : REACH + x_size, ROWS : ROWS + y_size] = passive[...]
    s_out[REACH : REACH + x_size, ROWS : ROWS + y_size] = support[...]
    pl.semaphore_wait(barrier, met)

    def copies(dx, dy, slot, chosen):
        made = []
        fields = [
            (design, d_out, deep, deep, ROWS, ROWS, False),
            (passive, p_out, REACH, REACH, ROWS, ROWS, False),
            (support, s_out, REACH, REACH, ROWS, ROWS, False),
            (few, few, BELOW, ABOVE, BELOW, ABOVE, True),
            (w_out, w_out, BELOW, ABOVE, BELOW, ABOVE, True),
        ]
        for at, (source, target, xb, xa, yb, ya, packed) in enumerate(fields):
            if at not in chosen:
                continue
            xs, xd, xn = part_of(-dx, x_size, xb, xa)
            ys, yd, yn = part_of(-dy, y_size, yb, ya)
            if xn <= 0 or yn <= 0:
                continue
            if packed:
                xs, ys = xs + BELOW, ys + BELOW
            made.append(
                pltpu.make_async_remote_copy(
                    src_ref=source.at[pl.ds(xs, xn), pl.ds(ys, yn)],
                    dst_ref=target.at[pl.ds(xd, xn), pl.ds(yd, yn)],
                    send_sem=send.at[slot, at],
                    recv_sem=recv.at[slot, at],
                    device_id=(gx + dx, yz + dy),
                    device_id_type=MESH,
                )
            )
        return made

    def start(chosen):
        for slot, (dx, dy) in enumerate(offsets):

            @pl.when(there(dx, dy))
            def _():
                for copy in copies(dx, dy, slot, chosen):
                    copy.start()

    def arrived(chosen):
        for slot, (dx, dy) in enumerate(offsets):

            @pl.when(there(-dx, -dy))
            def _():
                for copy in copies(dx, dy, slot, chosen):
                    copy.wait_recv()

    start((0, 1, 2))
    start((3,))
    pack(w_out, 0, full)
    start((4,))
    arrived((0, 1, 2))
    filter_density(counts, sizes, d_out, p_out, s_out, fa, fb, dens, mod, scale)
    arrived((3,))
    filter_modes, elements, force = block_ops(sizes, scale, mod, y0, y1, us, ud, fs, fd)
    filter_modes(1, rest, few)
    elements(1, BELOW, BELOW + x_size, BELOW, BELOW + y_size)

    @pl.loop(0, x_size + 1)
    def _(i):
        for j in range(y_size + 1):
            for c in range(3):
                y2_out[i, j, c] = y0[0, i + BELOW, j + BELOW, c]
                force_out[i, j, c] = force(0, i + BELOW, j + BELOW, c)

    arrived((4,))
    for slot, (dx, dy) in enumerate(offsets):

        @pl.when(there(dx, dy))
        def _():
            for copy in copies(dx, dy, slot, (0, 1, 2, 3, 4)):
                copy.wait_send()


def block_kernel(counts, sizes, modes, w_in, mod, scale, y2_in, force_in, y2_out, scale_out, sums_out, y0, y1, us, ud, fs, fd):
    x_size, y_size = sizes
    depth = scale.shape[-1]
    f32 = jnp.float32
    tile = (HALF, depth)
    lane = lax.broadcasted_iota(jnp.int32, tile, 1)
    halves = -(-modes // HALF)
    x_total, y_total = counts[0] * x_size, counts[1] * y_size
    filter_modes, elements, force = block_ops(sizes, scale, mod, y0, y1, us, ud, fs, fd)
    scale_out[...] = scale[REACH : REACH + x_size, ROWS : ROWS + y_size]

    @pl.loop(0, x_size + 1)
    def _(i):
        for j in range(y_size + 1):
            at = j + ROWS
            sc = jnp.broadcast_to(scale[i + REACH, at : at + 1, :], tile)
            for c in range(3):
                value = y2_in[i, j, c]
                y0[halves - 1, i + BELOW, j + BELOW, c] = value
                y1[halves - 1, i + BELOW, j + BELOW, c] = sc * value
                us[halves - 1, i + BELOW, j + BELOW, c] = force_in[i, j, c]

    if halves > 1:
        filter_modes(halves - 1, HALF, w_in)
    if halves > 1:
        elements(halves - 1, BELOW, BELOW + x_size, BELOW, BELOW + y_size)

    y2_out[...] = y0[:, BELOW : BELOW + x_size, BELOW : BELOW + y_size]

    def pairs(i_count, j_count, right, left):
        def body(i, total):
            total = list(total)
            for j in range(BELOW, BELOW + j_count):
                for c in range(3):
                    values = [left(h, i, j, c) for h in range(halves)]
                    for m in range(modes):
                        other = jnp.broadcast_to(right[m // HALF, i, j, c, m % HALF : m % HALF + 1, :], tile)
                        for h in range(halves):
                            total[m * halves + h] = total[m * halves + h] + values[h] * other
            return tuple(total)

        return lax.fori_loop(BELOW, BELOW + i_count, body, (jnp.zeros(tile, f32),) * (modes * halves))

    gram = pairs(x_size, y_size, y0, lambda h, i, j, c: y0[h, i, j, c])
    for h in range(halves):
        out = jnp.zeros(tile, f32)
        for m in range(modes):
            out = jnp.where(lane == m, jnp.sum(gram[m * halves + h], axis=1, keepdims=True), out)
        sums_out[h] = out

    @pl.loop(BELOW, BELOW + x_size + 1)
    def _(i):
        for j in range(BELOW, BELOW + y_size + 1):
            for h in range(halves - 1):
                for c in range(3):
                    us[h, i, j, c] = force(h, i, j, c)

    stiff = pairs(x_size + 1, y_size + 1, y1, lambda h, i, j, c: us[h, i, j, c])
    for h in range(halves):
        out = sums_out[h]
        for m in range(modes):
            out = jnp.where(lane == 32 + m, jnp.sum(stiff[m * halves + h], axis=1, keepdims=True), out)
        sums_out[h] = out * (1.0 / (3.0 * x_total * y_total * depth))


def sum_kernel(counts, part, out, first, second, send, recv):
    gx, yz = lax.axis_index("gx"), lax.axis_index("yz")
    barrier = pltpu.get_barrier_semaphore()
    x_count, y_count = counts
    for d in range(1, x_count):
        pl.semaphore_signal(barrier, inc=1, device_id=(lax.rem(gx + d, x_count), yz), device_id_type=MESH)
    for d in range(1, y_count):
        pl.semaphore_signal(barrier, inc=1, device_id=(gx, lax.rem(yz + d, y_count)), device_id_type=MESH)
    first[gx] = part[...]
    pl.semaphore_wait(barrier, x_count + y_count - 2)

    def gather(slots, me, count, device, base):
        sent = []
        for d in range(1, count):
            copy = pltpu.make_async_remote_copy(
                src_ref=slots.at[me],
                dst_ref=slots.at[me],
                send_sem=send.at[base + d],
                recv_sem=recv.at[base + d],
                device_id=device(lax.rem(me + d, count)),
                device_id_type=MESH,
            )
            copy.start()
            sent.append(copy)
        for d in range(1, count):
            source = lax.rem(me + count - d, count)
            pltpu.make_async_remote_copy(
                src_ref=slots.at[source],
                dst_ref=slots.at[source],
                send_sem=send.at[base + d],
                recv_sem=recv.at[base + d],
                device_id=device(source),
                device_id_type=MESH,
            ).wait_recv()
        for copy in sent:
            copy.wait_send()
        total = slots[0]
        for k in range(1, count):
            total = total + slots[k]
        return total

    if x_count > 1:
        second[yz] = gather(first, gx, x_count, lambda k: (k, yz), 0)
    else:
        second[yz] = first[0]
    out[...] = gather(second, yz, y_count, lambda k: (gx, k), x_count) if y_count > 1 else second[0]


def finish_kernel(sizes, modes, sums, y2, scale, shapes, projected):
    x_size, y_size = sizes
    depth = y2.shape[-1]
    halves = y2.shape[0]
    rows = halves * HALF
    f32 = jnp.float32
    sub = lax.broadcasted_iota(jnp.int32, (rows, depth), 0)
    lane = lax.broadcasted_iota(jnp.int32, (rows, depth), 1)
    work = sums[...].reshape(rows, depth)
    work = jnp.where((lane < 64) & (sub < modes), work, 0.0)
    work = jnp.where((lane == sub + 64) & (sub < modes), 1.0, work)
    for k in range(modes):
        column = jnp.sum(jnp.where(lane == k, work, 0.0), axis=1, keepdims=True)
        row = work[k : k + 1, :]
        root = 1.0 / jnp.sqrt(column[k : k + 1, :])
        row = row * root
        work = jnp.where(sub == k, row, work - jnp.where(sub > k, column * root, 0.0) * row)
    inverse = jnp.where(lane < modes, pltpu.roll(work, depth - 64, 1), 0.0)
    half_done = jnp.where(lane < modes, pltpu.roll(work, depth - 32, 1), 0.0)
    product = lax.dot_general(
        half_done, inverse, (((1,), (1,)), ((), ())), precision=lax.Precision.HIGHEST, preferred_element_type=f32
    )
    projected[...] = product[:modes, :modes]
    columns = []
    for m in range(modes):
        column = jnp.sum(jnp.where(lane == m, inverse, 0.0), axis=1, keepdims=True)
        for h in range(halves):
            columns.append(jnp.broadcast_to(column[h * HALF : (h + 1) * HALF], (HALF, depth)))
    stride = x_size * y_size

    @pl.loop(0, x_size)
    def _(x):
        for y in range(y_size):
            sc = jnp.broadcast_to(scale[x, y : y + 1, :], (HALF, depth))
            for c in range(3):
                total = [jnp.zeros((HALF, depth), f32)] * halves
                for m in range(modes):
                    one = jnp.broadcast_to(y2[m // HALF, x, y, c, m % HALF : m % HALF + 1, :], (HALF, depth))
                    for h in range(m // HALF, halves):
                        total[h] = total[h] + columns[m * halves + h] * one
                for h in range(halves):
                    count = min(HALF, modes - h * HALF)
                    at = (c * modes + h * HALF) * stride + x * y_size + y
                    shapes[pl.ds(at, count, stride=stride), :] = (sc * total[h])[:count]


def on_device(counts, design, passive, support, warm_modes):
    x_size, y_size, depth = design.shape
    sizes = (x_size, y_size)
    modes = warm_modes.shape[1]
    halves = -(-modes // HALF)
    rest = modes - (halves - 1) * HALF
    deep = SWEEPS + REACH
    f32 = jnp.float32
    rows = y_size + 2 * ROWS
    x_nodes, y_nodes = x_size + BELOW + ABOVE, y_size + BELOW + ABOVE
    slots = len(offsets_of(x_size))
    warm = warm_modes.reshape(3 * modes * x_size * y_size, depth)
    whole_rows = 3 * (modes - rest)
    field = pltpu.VMEM((x_size + 2 * deep, rows, depth), f32)
    short = (x_size + 2 * REACH, rows, depth)
    one = pltpu.VMEM((1, x_nodes, y_nodes, 3, HALF, depth), f32)
    block = pltpu.VMEM((halves, x_nodes, y_nodes, 3, HALF, depth), f32)
    middle = pl.pallas_call(
        functools.partial(exchange_kernel, counts, sizes, modes),
        out_shape=(
            jax.ShapeDtypeStruct((x_nodes, y_nodes, whole_rows, depth), f32),
            jax.ShapeDtypeStruct(short, f32),
            jax.ShapeDtypeStruct(short, f32),
            jax.ShapeDtypeStruct((x_size + 1, y_size + 1, 3, HALF, depth), f32),
            jax.ShapeDtypeStruct((x_size + 1, y_size + 1, 3, HALF, depth), f32),
        ),
        in_specs=[VMEM] * 4,
        out_specs=(VMEM,) * 5,
        scratch_shapes=[
            pltpu.VMEM((x_nodes, y_nodes, 3 * rest, depth), f32),
            field,
            pltpu.VMEM(short, jnp.int32),
            pltpu.VMEM(short, jnp.int32),
            field,
            field,
            pltpu.VMEM(short, f32),
        ]
        + [one] * 6
        + [pltpu.SemaphoreType.DMA((slots, 5)), pltpu.SemaphoreType.DMA((slots, 5))],
        compiler_params=pltpu.CompilerParams(collective_id=0, has_side_effects=True, vmem_limit_bytes=LIMIT),
        name="exchange_and_filter",
    )(design, passive, support, warm)
    y2, scale, sums = pl.pallas_call(
        functools.partial(block_kernel, counts, sizes, modes),
        out_shape=(
            jax.ShapeDtypeStruct((halves, x_size, y_size, 3, HALF, depth), f32),
            jax.ShapeDtypeStruct((x_size, y_size, depth), f32),
            jax.ShapeDtypeStruct((halves, HALF, depth), f32),
        ),
        in_specs=[VMEM] * 5,
        out_specs=(VMEM,) * 3,
        scratch_shapes=[block] * 6,
        compiler_params=pltpu.CompilerParams(vmem_limit_bytes=LIMIT),
        name="filter_block",
    )(*middle)
    total = pl.pallas_call(
        functools.partial(sum_kernel, counts),
        out_shape=jax.ShapeDtypeStruct(sums.shape, f32),
        in_specs=[VMEM],
        out_specs=VMEM,
        scratch_shapes=[
            pltpu.VMEM((counts[0],) + sums.shape, f32),
            pltpu.VMEM((counts[1],) + sums.shape, f32),
            pltpu.SemaphoreType.DMA((counts[0] + counts[1],)),
            pltpu.SemaphoreType.DMA((counts[0] + counts[1],)),
        ],
        compiler_params=pltpu.CompilerParams(collective_id=1, has_side_effects=True),
        name="sum_grams",
    )(sums)
    shapes, projected = pl.pallas_call(
        functools.partial(finish_kernel, sizes, modes),
        out_shape=(
            jax.ShapeDtypeStruct(warm.shape, f32),
            jax.ShapeDtypeStruct((modes, modes), f32),
        ),
        in_specs=[VMEM] * 3,
        out_specs=(VMEM, VMEM),
        compiler_params=pltpu.CompilerParams(vmem_limit_bytes=LIMIT),
        name="orthonormal_shapes",
    )(total, y2, scale)
    return shapes.reshape(warm_modes.shape), projected


def solution(mesh):
    counts = (mesh.shape["gx"], mesh.shape["yz"])
    return jax.shard_map(
        functools.partial(on_device, counts),
        mesh=mesh,
        in_specs=(
            P("gx", "yz", None),
            P("gx", "yz", None),
            P("gx", "yz", None),
            P(None, None, "gx", "yz", None),
        ),
        out_specs=(P(None, None, "gx", "yz", None), P()),
        check_vma=False,
    )
```

```python
import functools

import jax
import jax.numpy as jnp
import numpy as np
from jax import lax
from jax.experimental import pallas as pl
from jax.experimental.pallas import tpu as pltpu
from jax.sharding import PartitionSpec as P

SWEEPS = 4
SOFT = 0.001
CUT = 0.02
MESH = pl.DeviceIdType.MESH
VMEM = pl.BlockSpec(memory_space=pltpu.VMEM)
HALF = 8
ROWS = 8
REACH = 3
BELOW = 2
ABOVE = 3
LIMIT = 60 * 1024 * 1024


def element_matrix():
    poisson = 0.3
    lame_first = poisson / ((1.0 + poisson) * (1.0 - 2.0 * poisson))
    lame_shear = 0.5 / (1.0 + poisson)
    elastic = np.zeros((6, 6))
    elastic[:3, :3] = lame_first
    for direction in range(3):
        elastic[direction, direction] += 2.0 * lame_shear
        elastic[direction + 3, direction + 3] = lame_shear
    corner_signs = (
        np.array(
            [
                [a_side, b_side, c_side]
                for a_side in (0, 1)
                for b_side in (0, 1)
                for c_side in (0, 1)
            ]
        )
        * 2.0
        - 1.0
    )
    gauss_points = np.array([-1.0, 1.0]) / np.sqrt(3.0)
    stiffness = np.zeros((24, 24))
    for first_point in gauss_points:
        for second_point in gauss_points:
            for third_point in gauss_points:
                natural = np.array([first_point, second_point, third_point])
                gradients = np.zeros((8, 3))
                for corner in range(8):
                    for direction in range(3):
                        product = corner_signs[corner, direction] / 8.0
                        for other in range(3):
                            if other != direction:
                                product = product * (
                                    1.0 + corner_signs[corner, other] * natural[other]
                                )
                        gradients[corner, direction] = 2.0 * product
                strain = np.zeros((6, 24))
                for corner in range(8):
                    strain[0, corner] = gradients[corner, 0]
                    strain[1, 8 + corner] = gradients[corner, 1]
                    strain[2, 16 + corner] = gradients[corner, 2]
                    strain[3, corner] = gradients[corner, 1]
                    strain[3, 8 + corner] = gradients[corner, 0]
                    strain[4, 8 + corner] = gradients[corner, 2]
                    strain[4, 16 + corner] = gradients[corner, 1]
                    strain[5, corner] = gradients[corner, 2]
                    strain[5, 16 + corner] = gradients[corner, 0]
                stiffness = stiffness + strain.T @ elastic @ strain * 0.125
    return stiffness


def upper_value():
    return 8.0 * float(np.max(np.sum(np.abs(element_matrix()), axis=1)))


def edges():
    upper = upper_value()
    lower = CUT * upper
    return 0.5 * (upper + lower), 0.5 * (upper - lower)


def part_of(offset, size, before, after):
    first = max(offset * size, -before)
    stop = min(offset * size + size, size + after)
    return first - offset * size, first + before, stop - first


def offsets_of(x_size):
    hops = -(-(SWEEPS + REACH) // x_size)
    found = []
    for dx in range(-hops, hops + 1):
        for dy in (-1, 0, 1):
            if (dx, dy) != (0, 0):
                found.append((dx, dy))
    return found


def filter_density(counts, sizes, d_in, p_in, s_in, fa, fb, dens, mod, scale):
    x_size, y_size = sizes
    depth = d_in.shape[-1]
    x_start, y_start = lax.axis_index("gx") * x_size, lax.axis_index("yz") * y_size
    x_total, y_total = counts[0] * x_size, counts[1] * y_size
    deep = SWEEPS + REACH
    rows = y_size + 2 * ROWS
    row_at = lax.broadcasted_iota(jnp.int32, (rows, depth), 0) + (y_start - ROWS)
    lane_at = lax.broadcasted_iota(jnp.int32, (rows, depth), 1)
    y_in = (row_at >= 0) & (row_at < y_total)
    f32 = jnp.float32

    def one(flag):
        return jnp.where(flag, f32(1.0), f32(0.0))

    yz_part = one(row_at > 0) + one(row_at < y_total - 1) + one(lane_at > 0) + one(lane_at < depth - 1)

    def inside(x):
        return y_in & ((x >= 0) & (x < x_total))

    planes = x_size + 2 * deep

    @pl.loop(0, planes)
    def _(p):
        fa[p] = jnp.where(inside(x_start - deep + p), d_in[p], 0.0)

    for sweep in range(SWEEPS):
        old, new = (fa, fb) if sweep % 2 == 0 else (fb, fa)

        @pl.loop(sweep + 1, planes - sweep - 1)
        def _(p):
            x = x_start - deep + p
            here = old[p]
            around = old[p - 1] + old[p + 1]
            around = around + pltpu.roll(here, 1, 0) + pltpu.roll(here, rows - 1, 0)
            around = around + jnp.where(lane_at > 0, pltpu.roll(here, 1, 1), 0.0)
            around = around + jnp.where(lane_at < depth - 1, pltpu.roll(here, depth - 1, 1), 0.0)
            x_part = jnp.where(x > 0, f32(1.0), f32(0.0)) + jnp.where(x < x_total - 1, f32(1.0), f32(0.0))
            value = (d_in[p] + 2.0 * around) / (1.0 + 2.0 * (x_part + yz_part))
            new[p] = jnp.where(inside(x), value, 0.0)

    last = fa if SWEEPS % 2 == 0 else fb

    @pl.loop(0, x_size + 2 * REACH)
    def _(q):
        x = x_start - REACH + q
        ok = inside(x)
        value = jnp.where(p_in[q] == 1, f32(1.0), last[q + SWEEPS])
        dens[q] = jnp.where(ok, value, 0.0)
        mod[q] = jnp.where(ok, SOFT + (1.0 - SOFT) * (value * value * value), 0.0)

    @pl.loop(1, x_size + 2 * REACH)
    def _(q):
        x = x_start - REACH + q
        pair = dens[q - 1] + dens[q]
        pair = pair + pltpu.roll(pair, 1, 0)
        pair = pair + jnp.where(lane_at > 0, pltpu.roll(pair, 1, 1), 0.0)
        ok = inside(x) & (s_in[q] == 0)
        scale[q] = jnp.where(ok, 1.0 / jnp.sqrt(jnp.where(ok, pair, 8.0) * 0.125), 0.0)


def block_ops(sizes, scale, mod, y0, y1, us, ud, fs, fd):
    x_size, y_size = sizes
    depth = scale.shape[-1]
    f32 = jnp.float32
    tile = (HALF, depth)
    lane = lax.broadcasted_iota(jnp.int32, tile, 1)
    sub = lax.broadcasted_iota(jnp.int32, tile, 0)
    x_nodes, y_nodes = x_size + BELOW + ABOVE, y_size + BELOW + ABOVE
    to_row = ROWS - BELOW
    to_plane = REACH - BELOW

    def scale_at(i, j):
        return jnp.broadcast_to(scale[i + to_plane, j + to_row : j + to_row + 1, :], tile)

    def ahead(value):
        return jnp.where(lane < depth - 1, pltpu.roll(value, depth - 1, 1), 0.0)

    def behind(value):
        return jnp.where(lane > 0, pltpu.roll(value, 1, 1), 0.0)

    def put_scaled(h, i, j, c, u):
        after = ahead(u)
        us[h, i, j, c] = u + after
        ud[h, i, j, c] = after - u

    poisson = 0.3
    lam = poisson / ((1.0 + poisson) * (1.0 - 2.0 * poisson))
    mu = 0.5 / (1.0 + poisson)
    w0, w1, w2 = 1.0 / 16.0, 1.0 / 48.0, 1.0 / 144.0

    def elements(groups, i0, i1, j0, j1):
        def plane(h, i):
            def x_pairs(j):
                found = []
                for c in range(3):
                    s0, s1 = us[h, i, j, c], us[h, i + 1, j, c]
                    d0, d1 = ud[h, i, j, c], ud[h, i + 1, j, c]
                    found += [s0 + s1, s1 - s0, d0 + d1, d1 - d0]
                return found

            def put(j, part):
                for c in range(3):
                    ss, ds, sd, dd = part[4 * c : 4 * c + 4]
                    fs[h, i, j, c] = fs[h, i, j, c] + (ss - ds)
                    fd[h, i, j, c] = fd[h, i, j, c] + (sd - dd)
                    fs[h, i + 1, j, c] = ss + ds
                    fd[h, i + 1, j, c] = sd + dd

            def column(j, carry):
                low, above = carry[:12], carry[12:]
                high = x_pairs(j + 1)
                e = jnp.broadcast_to(mod[i + to_plane, j + to_row : j + to_row + 1, :], tile)
                u = []
                for c in range(3):
                    now = {}
                    for at, (xb, zb) in enumerate(((0, 0), (1, 0), (0, 1), (1, 1))):
                        p, q = low[4 * c + at], high[4 * c + at]
                        now[xb, 0, zb] = q + p
                        now[xb, 1, zb] = q - p
                    u.append(now)
                a, b, w = u
                fa_, fb_, fw_ = {}, {}, {}
                e_shear = e * (mu * w0)
                e_twice = e * (2.0 * mu * w0)
                x_, y_, z_ = (1, 0, 0), (0, 1, 0), (0, 0, 1)
                xy, xz, yz, xyz = (1, 1, 0), (1, 0, 1), (0, 1, 1), (1, 1, 1)
                trace = (e * (lam * w0)) * (a[x_] + b[y_] + w[z_])
                fa_[x_] = trace + e_twice * a[x_]
                fb_[y_] = trace + e_twice * b[y_]
                fw_[z_] = trace + e_twice * w[z_]
                fa_[y_] = fb_[x_] = e_shear * (a[y_] + b[x_])
                fa_[z_] = fw_[x_] = e_shear * (a[z_] + w[x_])
                fb_[z_] = fw_[y_] = e_shear * (b[z_] + w[y_])
                e_plus = e * ((2.0 * lam + 3.0 * mu) * w1 * 0.5)
                e_minus = e * (3.0 * mu * w1 * 0.5)
                for f1, k1, f2, k2, v1, v2 in (
                    (fa_, xy, fw_, yz, a[xy], w[yz]),
                    (fa_, xz, fb_, yz, a[xz], b[yz]),
                    (fb_, xy, fw_, xz, b[xy], w[xz]),
                ):
                    plus, minus = e_plus * (v1 + v2), e_minus * (v1 - v2)
                    f1[k1], f2[k2] = plus + minus, plus - minus
                e_mixed = e * (mu * w1)
                total = a[yz] + b[xz] + w[xy]
                fa_[yz] = e_mixed * (total + a[yz])
                fb_[xz] = e_mixed * (total + b[xz])
                fw_[xy] = e_mixed * (total + w[xy])
                e_last = e * ((lam + 4.0 * mu) * w2)
                for f, v in ((fa_, a), (fb_, b), (fw_, w)):
                    f[xyz] = e_last * v[xyz]
                part, rest = [], []
                for c, f in enumerate((fa_, fb_, fw_)):
                    for at, (xb, zb) in enumerate(((0, 0), (1, 0), (0, 1), (1, 1))):
                        odd = f[xb, 1, zb]
                        if (xb, zb) == (0, 0):
                            part.append(above[4 * c + at] - odd)
                            rest.append(odd)
                        else:
                            even = f[xb, 0, zb]
                            part.append(above[4 * c + at] + (even - odd))
                            rest.append(even + odd)
                put(j, part)
                return tuple(high) + tuple(rest)

            zero = jnp.zeros(tile, f32)
            carry = tuple(x_pairs(j0)) + (zero,) * 12
            for j in range(j0, j1):
                carry = column(j, carry)
            put(j1, carry[12:])

        @pl.loop(0, groups)
        def _(h):
            for j in range(j0, j1 + 1):
                for c in range(3):
                    fs[h, i0, j, c] = jnp.zeros(tile, f32)
                    fd[h, i0, j, c] = jnp.zeros(tile, f32)

            @pl.loop(i0, i1)
            def _(i):
                plane(h, i)

    def force(h, i, j, c):
        s, d = fs[h, i, j, c], fd[h, i, j, c]
        return (s - d) + behind(s + d)

    def filter_modes(groups, count, w_in):
        @pl.loop(0, x_nodes)
        def _(i):
            for j in range(y_nodes):
                sc = scale_at(i, j)
                for h in range(groups):
                    keep = (sc > 0.0) & (sub < count)
                    for c in range(3):
                        first = c * count
                        begin = min(first, 3 * count - HALF)
                        value = w_in[i, j, begin : begin + HALF, :]
                        if begin != first:
                            value = pltpu.roll(value, HALF - (first - begin), 0)
                        value = jnp.where(keep, value, 0.0)
                        y0[h, i, j, c] = value
                        put_scaled(h, i, j, c, sc * value)

        center, width = edges()
        elements(groups, 0, x_nodes - 1, 0, y_nodes - 1)

        @pl.loop(1, x_nodes - 1)
        def _(i):
            for j in range(1, y_nodes - 1):
                sc = scale_at(i, j)
                to = sc * (1.0 / width)
                for h in range(groups):
                    for c in range(3):
                        value = to * force(h, i, j, c) - (center / width) * y0[h, i, j, c]
                        y1[h, i, j, c] = value
                        put_scaled(h, i, j, c, sc * value)

        elements(groups, 1, x_nodes - 2, 1, y_nodes - 2)

        @pl.loop(BELOW, BELOW + x_size + 1)
        def _(i):
            for j in range(BELOW, BELOW + y_size + 1):
                sc = scale_at(i, j)
                to = sc * (2.0 / width)
                for h in range(groups):
                    for c in range(3):
                        value = to * force(h, i, j, c) - (2.0 * center / width) * y1[h, i, j, c] - y0[h, i, j, c]
                        y0[h, i, j, c] = value
                        y1[h, i, j, c] = sc * value
                        put_scaled(h, i, j, c, sc * value)

    return filter_modes, elements, force


def exchange_kernel(counts, sizes, modes, design, passive, support, warm, w_out, mod, scale, y2_out, force_out, few, d_out, p_out, s_out, fa, fb, dens, y0, y1, us, ud, fs, fd, send, recv):
    x_size, y_size = sizes
    full = modes // HALF * HALF
    if full == modes:
        full = modes - HALF
    rest = modes - full
    gx, yz = lax.axis_index("gx"), lax.axis_index("yz")
    offsets = offsets_of(x_size)
    deep = SWEEPS + REACH

    def there(dx, dy):
        x, y = gx + dx, yz + dy
        return (x >= 0) & (x < counts[0]) & (y >= 0) & (y < counts[1])

    barrier = pltpu.get_barrier_semaphore()
    met = jnp.int32(0)
    for dx, dy in offsets:
        ok = there(dx, dy)
        met = met + ok.astype(jnp.int32)

        @pl.when(ok)
        def _():
            pl.semaphore_signal(barrier, inc=1, device_id=(gx + dx, yz + dy), device_id_type=MESH)

    stride = x_size * y_size

    def pack(target, first, count):
        for x in range(x_size):
            for y in range(y_size):
                for c in range(3):
                    begin = (c * modes + first) * stride + x * y_size + y
                    target[x + BELOW, y + BELOW, c * count : (c + 1) * count] = warm[pl.ds(begin, count, stride=stride), :]

    pack(few, full, rest)
    d_out[deep : deep + x_size, ROWS : ROWS + y_size] = design[...]
    p_out[REACH : REACH + x_size, ROWS : ROWS + y_size] = passive[...]
    s_out[REACH : REACH + x_size, ROWS : ROWS + y_size] = support[...]
    pl.semaphore_wait(barrier, met)

    def copies(dx, dy, slot, chosen, piece=None):
        made = []
        fields = [
            (design, d_out, deep, deep, ROWS, ROWS, False),
            (passive, p_out, REACH, REACH, ROWS, ROWS, False),
            (support, s_out, REACH, REACH, ROWS, ROWS, False),
            (few, few, BELOW, ABOVE, BELOW, ABOVE, True),
            (w_out, w_out, BELOW, ABOVE, BELOW, ABOVE, True),
        ]
        for at, (source, target, xb, xa, yb, ya, packed) in enumerate(fields):
            if at not in chosen:
                continue
            xs, xd, xn = part_of(-dx, x_size, xb, xa)
            ys, yd, yn = part_of(-dy, y_size, yb, ya)
            if piece is not None:
                xs, xd, xn = xs + piece, xd + piece, min(1, xn - piece)
            if xn <= 0 or yn <= 0:
                continue
            if packed:
                xs, ys = xs + BELOW, ys + BELOW
            made.append(
                pltpu.make_async_remote_copy(
                    src_ref=source.at[pl.ds(xs, xn), pl.ds(ys, yn)],
                    dst_ref=target.at[pl.ds(xd, xn), pl.ds(yd, yn)],
                    send_sem=send.at[slot, at],
                    recv_sem=recv.at[slot, at],
                    device_id=(gx + dx, yz + dy),
                    device_id_type=MESH,
                )
            )
        return made

    def start(chosen):
        for slot, (dx, dy) in enumerate(offsets):

            @pl.when(there(dx, dy))
            def _():
                for copy in copies(dx, dy, slot, chosen):
                    copy.start()

    def start_planes(chosen):
        order = sorted(enumerate(offsets), key=lambda item: abs(item[1][0]) + abs(item[1][1]))
        for piece in range(max(x_size, BELOW, ABOVE)):
            for slot, (dx, dy) in order:
                if part_of(-dx, x_size, BELOW, ABOVE)[2] > piece:

                    @pl.when(there(dx, dy))
                    def _():
                        for copy in copies(dx, dy, slot, chosen, piece):
                            copy.start()

    def arrived(chosen):
        for slot, (dx, dy) in enumerate(offsets):

            @pl.when(there(-dx, -dy))
            def _():
                for copy in copies(dx, dy, slot, chosen):
                    copy.wait_recv()

    start((0, 1, 2))
    start_planes((3,))
    pack(w_out, 0, full)
    start_planes((4,))
    arrived((0, 1, 2))
    filter_density(counts, sizes, d_out, p_out, s_out, fa, fb, dens, mod, scale)
    arrived((3,))
    filter_modes, elements, force = block_ops(sizes, scale, mod, y0, y1, us, ud, fs, fd)
    filter_modes(1, rest, few)
    elements(1, BELOW, BELOW + x_size, BELOW, BELOW + y_size)

    @pl.loop(0, x_size + 1)
    def _(i):
        for j in range(y_size + 1):
            for c in range(3):
                y2_out[i, j, c] = y0[0, i + BELOW, j + BELOW, c]
                force_out[i, j, c] = force(0, i + BELOW, j + BELOW, c)

    arrived((4,))
    for slot, (dx, dy) in enumerate(offsets):

        @pl.when(there(dx, dy))
        def _():
            for copy in copies(dx, dy, slot, (0, 1, 2, 3, 4)):
                copy.wait_send()


def block_kernel(counts, sizes, modes, w_in, mod, scale, y2_in, force_in, y2_out, scale_out, sums_out, y0, y1, us, ud, fs, fd):
    x_size, y_size = sizes
    depth = scale.shape[-1]
    f32 = jnp.float32
    tile = (HALF, depth)
    lane = lax.broadcasted_iota(jnp.int32, tile, 1)
    halves = -(-modes // HALF)
    x_total, y_total = counts[0] * x_size, counts[1] * y_size
    filter_modes, elements, force = block_ops(sizes, scale, mod, y0, y1, us, ud, fs, fd)
    scale_out[...] = scale[REACH : REACH + x_size, ROWS : ROWS + y_size]

    @pl.loop(0, x_size + 1)
    def _(i):
        for j in range(y_size + 1):
            at = j + ROWS
            sc = jnp.broadcast_to(scale[i + REACH, at : at + 1, :], tile)
            for c in range(3):
                value = y2_in[i, j, c]
                y0[halves - 1, i + BELOW, j + BELOW, c] = value
                y1[halves - 1, i + BELOW, j + BELOW, c] = sc * value
                us[halves - 1, i + BELOW, j + BELOW, c] = force_in[i, j, c]

    if halves > 1:
        filter_modes(halves - 1, HALF, w_in)
    if halves > 1:
        elements(halves - 1, BELOW, BELOW + x_size, BELOW, BELOW + y_size)

    y2_out[...] = y0[:, BELOW : BELOW + x_size, BELOW : BELOW + y_size]

    def pairs(i_count, j_count, right, left):
        def body(i, total):
            total = list(total)
            for j in range(BELOW, BELOW + j_count):
                for c in range(3):
                    values = [left(h, i, j, c) for h in range(halves)]
                    for m in range(modes):
                        other = jnp.broadcast_to(right[m // HALF, i, j, c, m % HALF : m % HALF + 1, :], tile)
                        for h in range(halves):
                            total[m * halves + h] = total[m * halves + h] + values[h] * other
            return tuple(total)

        return lax.fori_loop(BELOW, BELOW + i_count, body, (jnp.zeros(tile, f32),) * (modes * halves))

    gram = pairs(x_size, y_size, y0, lambda h, i, j, c: y0[h, i, j, c])
    for h in range(halves):
        out = jnp.zeros(tile, f32)
        for m in range(modes):
            out = jnp.where(lane == m, jnp.sum(gram[m * halves + h], axis=1, keepdims=True), out)
        sums_out[h] = out

    @pl.loop(BELOW, BELOW + x_size + 1)
    def _(i):
        for j in range(BELOW, BELOW + y_size + 1):
            for h in range(halves - 1):
                for c in range(3):
                    us[h, i, j, c] = force(h, i, j, c)

    stiff = pairs(x_size + 1, y_size + 1, y1, lambda h, i, j, c: us[h, i, j, c])
    for h in range(halves):
        out = sums_out[h]
        for m in range(modes):
            out = jnp.where(lane == 32 + m, jnp.sum(stiff[m * halves + h], axis=1, keepdims=True), out)
        sums_out[h] = out * (1.0 / (3.0 * x_total * y_total * depth))


def sum_kernel(counts, part, out, first, second, send, recv):
    gx, yz = lax.axis_index("gx"), lax.axis_index("yz")
    barrier = pltpu.get_barrier_semaphore()
    x_count, y_count = counts
    for d in range(1, x_count):
        pl.semaphore_signal(barrier, inc=1, device_id=(lax.rem(gx + d, x_count), yz), device_id_type=MESH)
    for d in range(1, y_count):
        pl.semaphore_signal(barrier, inc=1, device_id=(gx, lax.rem(yz + d, y_count)), device_id_type=MESH)
    first[gx] = part[...]
    pl.semaphore_wait(barrier, x_count + y_count - 2)

    def gather(slots, me, count, device, base):
        sent = []
        for d in range(1, count):
            copy = pltpu.make_async_remote_copy(
                src_ref=slots.at[me],
                dst_ref=slots.at[me],
                send_sem=send.at[base + d],
                recv_sem=recv.at[base + d],
                device_id=device(lax.rem(me + d, count)),
                device_id_type=MESH,
            )
            copy.start()
            sent.append(copy)
        for d in range(1, count):
            source = lax.rem(me + count - d, count)
            pltpu.make_async_remote_copy(
                src_ref=slots.at[source],
                dst_ref=slots.at[source],
                send_sem=send.at[base + d],
                recv_sem=recv.at[base + d],
                device_id=device(source),
                device_id_type=MESH,
            ).wait_recv()
        for copy in sent:
            copy.wait_send()
        total = slots[0]
        for k in range(1, count):
            total = total + slots[k]
        return total

    if x_count > 1:
        second[yz] = gather(first, gx, x_count, lambda k: (k, yz), 0)
    else:
        second[yz] = first[0]
    out[...] = gather(second, yz, y_count, lambda k: (gx, k), x_count) if y_count > 1 else second[0]


def finish_kernel(sizes, modes, sums, y2, scale, shapes, projected):
    x_size, y_size = sizes
    depth = y2.shape[-1]
    halves = y2.shape[0]
    rows = halves * HALF
    f32 = jnp.float32
    sub = lax.broadcasted_iota(jnp.int32, (rows, depth), 0)
    lane = lax.broadcasted_iota(jnp.int32, (rows, depth), 1)
    work = sums[...].reshape(rows, depth)
    work = jnp.where((lane < 64) & (sub < modes), work, 0.0)
    work = jnp.where((lane == sub + 64) & (sub < modes), 1.0, work)
    for k in range(modes):
        column = jnp.sum(jnp.where(lane == k, work, 0.0), axis=1, keepdims=True)
        row = work[k : k + 1, :]
        root = 1.0 / jnp.sqrt(column[k : k + 1, :])
        row = row * root
        work = jnp.where(sub == k, row, work - jnp.where(sub > k, column * root, 0.0) * row)
    inverse = jnp.where(lane < modes, pltpu.roll(work, depth - 64, 1), 0.0)
    half_done = jnp.where(lane < modes, pltpu.roll(work, depth - 32, 1), 0.0)
    product = lax.dot_general(
        half_done, inverse, (((1,), (1,)), ((), ())), precision=lax.Precision.HIGHEST, preferred_element_type=f32
    )
    projected[...] = product[:modes, :modes]
    columns = []
    for m in range(modes):
        column = jnp.sum(jnp.where(lane == m, inverse, 0.0), axis=1, keepdims=True)
        for h in range(halves):
            columns.append(jnp.broadcast_to(column[h * HALF : (h + 1) * HALF], (HALF, depth)))
    stride = x_size * y_size

    @pl.loop(0, x_size)
    def _(x):
        for y in range(y_size):
            sc = jnp.broadcast_to(scale[x, y : y + 1, :], (HALF, depth))
            for c in range(3):
                total = [jnp.zeros((HALF, depth), f32)] * halves
                for m in range(modes):
                    one = jnp.broadcast_to(y2[m // HALF, x, y, c, m % HALF : m % HALF + 1, :], (HALF, depth))
                    for h in range(m // HALF, halves):
                        total[h] = total[h] + columns[m * halves + h] * one
                for h in range(halves):
                    count = min(HALF, modes - h * HALF)
                    at = (c * modes + h * HALF) * stride + x * y_size + y
                    shapes[pl.ds(at, count, stride=stride), :] = (sc * total[h])[:count]


def on_device(counts, design, passive, support, warm_modes):
    x_size, y_size, depth = design.shape
    sizes = (x_size, y_size)
    modes = warm_modes.shape[1]
    halves = -(-modes // HALF)
    rest = modes - (halves - 1) * HALF
    deep = SWEEPS + REACH
    f32 = jnp.float32
    rows = y_size + 2 * ROWS
    x_nodes, y_nodes = x_size + BELOW + ABOVE, y_size + BELOW + ABOVE
    slots = len(offsets_of(x_size))
    warm = warm_modes.reshape(3 * modes * x_size * y_size, depth)
    whole_rows = 3 * (modes - rest)
    field = pltpu.VMEM((x_size + 2 * deep, rows, depth), f32)
    short = (x_size + 2 * REACH, rows, depth)
    one = pltpu.VMEM((1, x_nodes, y_nodes, 3, HALF, depth), f32)
    block = pltpu.VMEM((halves, x_nodes, y_nodes, 3, HALF, depth), f32)
    middle = pl.pallas_call(
        functools.partial(exchange_kernel, counts, sizes, modes),
        out_shape=(
            jax.ShapeDtypeStruct((x_nodes, y_nodes, whole_rows, depth), f32),
            jax.ShapeDtypeStruct(short, f32),
            jax.ShapeDtypeStruct(short, f32),
            jax.ShapeDtypeStruct((x_size + 1, y_size + 1, 3, HALF, depth), f32),
            jax.ShapeDtypeStruct((x_size + 1, y_size + 1, 3, HALF, depth), f32),
        ),
        in_specs=[VMEM] * 4,
        out_specs=(VMEM,) * 5,
        scratch_shapes=[
            pltpu.VMEM((x_nodes, y_nodes, 3 * rest, depth), f32),
            field,
            pltpu.VMEM(short, jnp.int32),
            pltpu.VMEM(short, jnp.int32),
            field,
            field,
            pltpu.VMEM(short, f32),
        ]
        + [one] * 6
        + [pltpu.SemaphoreType.DMA((slots, 5)), pltpu.SemaphoreType.DMA((slots, 5))],
        compiler_params=pltpu.CompilerParams(collective_id=0, has_side_effects=True, vmem_limit_bytes=LIMIT),
        name="exchange_and_filter",
    )(design, passive, support, warm)
    y2, scale, sums = pl.pallas_call(
        functools.partial(block_kernel, counts, sizes, modes),
        out_shape=(
            jax.ShapeDtypeStruct((halves, x_size, y_size, 3, HALF, depth), f32),
            jax.ShapeDtypeStruct((x_size, y_size, depth), f32),
            jax.ShapeDtypeStruct((halves, HALF, depth), f32),
        ),
        in_specs=[VMEM] * 5,
        out_specs=(VMEM,) * 3,
        scratch_shapes=[block] * 6,
        compiler_params=pltpu.CompilerParams(vmem_limit_bytes=LIMIT),
        name="filter_block",
    )(*middle)
    total = pl.pallas_call(
        functools.partial(sum_kernel, counts),
        out_shape=jax.ShapeDtypeStruct(sums.shape, f32),
        in_specs=[VMEM],
        out_specs=VMEM,
        scratch_shapes=[
            pltpu.VMEM((counts[0],) + sums.shape, f32),
            pltpu.VMEM((counts[1],) + sums.shape, f32),
            pltpu.SemaphoreType.DMA((counts[0] + counts[1],)),
            pltpu.SemaphoreType.DMA((counts[0] + counts[1],)),
        ],
        compiler_params=pltpu.CompilerParams(collective_id=1, has_side_effects=True),
        name="sum_grams",
    )(sums)
    shapes, projected = pl.pallas_call(
        functools.partial(finish_kernel, sizes, modes),
        out_shape=(
            jax.ShapeDtypeStruct(warm.shape, f32),
            jax.ShapeDtypeStruct((modes, modes), f32),
        ),
        in_specs=[VMEM] * 3,
        out_specs=(VMEM, VMEM),
        compiler_params=pltpu.CompilerParams(vmem_limit_bytes=LIMIT),
        name="orthonormal_shapes",
    )(total, y2, scale)
    return shapes.reshape(warm_modes.shape), projected


def solution(mesh):
    counts = (mesh.shape["gx"], mesh.shape["yz"])
    return jax.shard_map(
        functools.partial(on_device, counts),
        mesh=mesh,
        in_specs=(
            P("gx", "yz", None),
            P("gx", "yz", None),
            P("gx", "yz", None),
            P(None, None, "gx", "yz", None),
        ),
        out_specs=(P(None, None, "gx", "yz", None), P()),
        check_vma=False,
    )
```
